512 devices in a mesh: nodes: 32 (over x_lo, z, core), tensor: 16 (over y, x_hi).
Axes of the slice: x: 4 (x_hi: 2, x_lo: 2; x = x_hi * 2 + x_lo), y: 8, z: 8, core: 2. Of those that a mesh axis runs over, the one named last changes fastest.
Arguments:
- node_states: bfloat16 [32768, 1024], P(('nodes', 'tensor')), may hold values from -6 to 6
- norm_gain: float32 [1024], replicated, may hold values from 0.1 to 1.9
- input_weight: bfloat16 [3072, 1024], P('tensor'), may hold values from -3 to 3, as said below
- output_weight: bfloat16 [1024, 1024], P('tensor'), may hold values from -0.1875 to 0.1875
- expander_bias: float32 [4, 16], P(None, 'tensor'), may hold values from 3 to 6
- local_blocks: int32 [128, 4], P('nodes'), may hold values from 0 to 127, as said below
- expander_source: int32 [4, 32768], P(None, 'nodes'), may hold values from 0 to 32767, as said below
Outputs:
- layer_output: bfloat16 [32768, 1024], P(('nodes', 'tensor'))
The draws below stay inside these ranges and needn't reach their ends.
Inputs may be any that keep to these rules, and one draw needn't show every extreme that they name: `local_blocks`: row g lists block g first, then 4 - 1 other distinct blocks among the 8 consecutive blocks that start at min(max(g - 4, 0), 120). `expander_source`: each of the 4 rows is a permutation of the 32768 nodes. With partitions of 1024 consecutive nodes, in every round exactly 32 nodes of any partition take their expander source from any given partition. `input_weight`: rows h * 3 * 64 onward hold head h's query, key and value rows in that order.
All inputs are finite; a program needn't handle non-finite values.
Results may differ from the reference program's by a relative error of at most 0.0051.
Values may be sent and summed in bfloat16 or wider, within the bound.
A program may use at most 64 MiB of HBM per device.

```python
import math
import jax
import jax.numpy as jnp
from jax import lax

D = 1024
HEAD = 64
BLOCK = 256
NEIGH = 4
ROUNDS = 4
BLOCKS_DEV = 4
HEADS = 16
ROWS_DEV = 1024
NODES = 32768
BLOCKS = 128


def draw_input_weight(key, part):
    key = jax.random.fold_in(key, 11)
    head_count = D // HEAD
    base_key = jax.random.fold_in(key, 0)
    base = jax.random.normal(base_key, (D, head_count, 3, HEAD), jnp.float32) * D ** (-0.5)
    return jnp.transpose(base.reshape(D, 3 * D), (1, 0)).astype(jnp.bfloat16)


def draw_local_blocks(key, part):
    key = jax.random.fold_in(key, 23)
    window = 2 * BLOCKS_DEV
    centre = jnp.arange(BLOCKS, dtype=jnp.int32)
    lowest = jnp.clip(centre - BLOCKS_DEV, 0, BLOCKS - window)
    orders = jax.vmap(lambda subkey: jax.random.permutation(subkey, window - 1))(jax.random.split(key, BLOCKS))
    picked = orders[:, :NEIGH - 1].astype(jnp.int32)
    offset = (centre - lowest)[:, None]
    others = lowest[:, None] + picked + (picked >= offset).astype(jnp.int32)
    return jnp.concatenate([centre[:, None], others], axis=1).astype(jnp.int32)


def draw_expander_source(key, part):
    key = jax.random.fold_in(key, 37)
    partitions = NODES // ROWS_DEV

    def one_round(round_key):
        order_key, source_key, target_key = jax.random.split(round_key, 3)
        relabel = jax.random.permutation(order_key, partitions).astype(jnp.int32)
        source_orders = jax.vmap(lambda subkey: jax.random.permutation(subkey, ROWS_DEV))(jax.random.split(source_key, partitions)).astype(jnp.int32)
        target_orders = jax.vmap(lambda subkey: jax.random.permutation(subkey, ROWS_DEV))(jax.random.split(target_key, partitions)).astype(jnp.int32)
        target = jnp.arange(partitions, dtype=jnp.int32)[:, None]
        slot_group = target_orders % partitions
        slot_rank = target_orders // partitions
        owner = relabel[(slot_group + target) % partitions]
        local_row = source_orders[owner, slot_rank * partitions + target]
        return (owner * ROWS_DEV + local_row).reshape(NODES)
    return jax.vmap(one_round)(jax.random.split(key, ROUNDS)).astype(jnp.int32)


def block_levels(own_key, extent, shards, low, high):
    gain = 1.0
    for axis_at, shards_of in shards:
        draws = jax.random.uniform(jax.random.fold_in(jax.random.fold_in(own_key, 6), axis_at), (shards_of,), jnp.float32, low / len(shards), high / len(shards))
        gain = gain * jnp.repeat(jnp.exp(draws), extent[axis_at] // shards_of).reshape((-1,) + (1,) * (len(extent) - 1 - axis_at))
    return gain


def noise(rng, extent, width, reach, shards=(), kind=jnp.bfloat16):
    values = jax.random.normal(rng, extent, jnp.float32) * width
    if len(shards) > 0:
        values = block_levels(rng, extent, shards, -0.22, 0.18) * values
    return jnp.clip(values, min=-reach, max=reach).astype(kind)


def setup_inputs(seed: int = 0) -> dict:
    streams_of = jax.random.split(jax.random.key(seed), 8)
    return {
        "node_states": noise(streams_of[0], (NODES, D), 1.0, 6.0, ((0, 512),)),
        "norm_gain": jnp.clip(1.0 + 0.18 * jax.random.normal(streams_of[1], (D,), jnp.float32), 0.1, 1.9),
        "input_weight": draw_input_weight(jax.random.fold_in(streams_of[7], 71), 0),
        "output_weight": noise(streams_of[3], (D, D), D ** -0.5, 0.1875, ((0, 16),)),
        "expander_bias": jnp.clip(3.0 + 3.0 * jax.random.uniform(streams_of[4], (ROUNDS, HEADS), jnp.float32) ** block_levels(streams_of[4], (ROUNDS, HEADS), ((1, 16),), -0.2, 0.2), 3.0, 6.0),
        "local_blocks": draw_local_blocks(jax.random.fold_in(streams_of[7], 71), 0),
        "expander_source": draw_expander_source(jax.random.fold_in(streams_of[7], 71), 0),
    }


def widened_round_output(values):
    rounded = lax.optimization_barrier(values.astype(jnp.bfloat16))
    return rounded.astype(jnp.float32)

def reference(node_states, norm_gain, input_weight, output_weight, expander_bias, local_blocks, expander_source):
    head_count = D // HEAD
    score_scale = 1.0 / math.sqrt(HEAD)
    states_wide = node_states.astype(jnp.float32)
    inverse_rms = lax.rsqrt(lax.optimization_barrier(jnp.sum(states_wide * states_wide, axis=1)) / D + 1e-05)
    scaled = (states_wide * norm_gain).astype(jnp.bfloat16)
    block_count = local_blocks.shape[0]

    def one_head(head_index):
        weights = lax.dynamic_slice_in_dim(input_weight, head_index * 3 * HEAD, 3 * HEAD, 0)
        projected = lax.dot_general(scaled, weights, (((1,), (1,)), ((), ())), preferred_element_type=jnp.float32) * inverse_rms[:, None]
        projected = projected.astype(jnp.bfloat16).reshape(-1, 3, HEAD)
        queries = projected[:, 0, :]
        keys_all = projected[:, 1, :]
        values_all = projected[:, 2, :]
        query_tiles_local = queries.reshape(block_count, BLOCK, HEAD).astype(jnp.float32)
        key_tiles_local = keys_all.reshape(block_count, BLOCK, HEAD)[local_blocks].astype(jnp.float32)
        value_tiles_local = values_all.reshape(block_count, BLOCK, HEAD)[local_blocks].astype(jnp.float32)
        nearby_scores = jnp.einsum('tvi,tpui->tvpu', query_tiles_local, key_tiles_local) * score_scale
        far_keys = keys_all[expander_source].astype(jnp.float32)
        distant_values = values_all[expander_source].astype(jnp.float32).reshape(ROUNDS, block_count, BLOCK, HEAD)
        bias_row = lax.dynamic_index_in_dim(expander_bias, head_index, 1, keepdims=False)
        scores_far = jnp.einsum('nd,rnd->nr', queries.astype(jnp.float32), far_keys) * score_scale + bias_row[None, :]
        scores_far = scores_far.reshape(block_count, BLOCK, ROUNDS)
        highest = jnp.maximum(lax.optimization_barrier(jnp.max(nearby_scores, axis=(2, 3))), lax.optimization_barrier(jnp.max(scores_far, axis=2)))
        exponent_nearby = jnp.exp(nearby_scores - highest[:, :, None, None])
        exponent_distant = jnp.exp(scores_far - highest[:, :, None])
        total = lax.optimization_barrier(jnp.sum(exponent_nearby, axis=(2, 3))) + lax.optimization_barrier(jnp.sum(exponent_distant, axis=2))
        blended_output = jnp.einsum('uoyw,uywr->uor', widened_round_output(exponent_nearby), value_tiles_local)
        blended_output = blended_output + jnp.einsum('uic,cuif->uif', widened_round_output(exponent_distant), distant_values)
        return (blended_output / total[:, :, None]).astype(jnp.bfloat16).reshape(-1, HEAD)
    per_head = lax.map(one_head, jnp.arange(head_count, dtype=jnp.int32))
    attended = jnp.transpose(per_head, (1, 0, 2)).reshape(-1, D)
    projected_out = jnp.dot(attended, output_weight, preferred_element_type=jnp.float32)
    return (states_wide + projected_out).astype(jnp.bfloat16)
```

```python
import functools
import math

import jax
import jax.numpy as jnp
from jax import lax
from jax.experimental import pallas as pl
from jax.experimental.pallas import tpu as pltpu
from jax.sharding import PartitionSpec as P

D = 1024
HEAD = 64
BLOCK = 256
NEIGH = 4
ROUNDS = 4
EPS = 1e-05

BF16 = jnp.bfloat16
F32 = jnp.float32
MESH = pl.DeviceIdType.MESH
NT = (((1,), (1,)), ((), ()))


def iota(shape, dim):
    return lax.broadcasted_iota(jnp.int32, shape, dim)


def kernel(
    parts,
    peers,
    x_ref,
    gain_ref,
    win_ref,
    wout_ref,
    bias_ref,
    blocks_ref,
    src_ref,
    out_ref,
    xg,
    kvx,
    qs,
    reqs,
    reqr,
    posr,
    pick,
    place,
    snd,
    rcv,
    far,
    oloc,
    mloc,
    lloc,
    att,
    atts,
    attr,
    woutg,
    x_send,
    x_recv,
    w_send,
    w_recv,
    c_send,
    c_recv,
    r_send,
    r_recv,
    e_send,
    e_recv,
    n_send,
    n_recv,
    a_send,
    a_recv,
):
    own = x_ref.shape[0]
    rows = own * peers
    ring = peers // 2
    per = rows // parts
    blocks_here = rows // BLOCK
    p = lax.axis_index("nodes")
    t = lax.axis_index("tensor")
    y, xh = t // 2, t % 2
    core = p % 2
    other_core = p + 1 - 2 * core

    def node_peer(d):
        return (p + d) % parts

    def tensor_peer(d):
        return (t + d) % peers

    barrier = pltpu.get_barrier_semaphore()

    @pl.loop(1, parts)
    def _(d):
        pl.semaphore_signal(barrier, inc=1, device_id={"nodes": node_peer(d)}, device_id_type=MESH)

    @pl.loop(1, peers)
    def _(d):
        pl.semaphore_signal(
            barrier, inc=1, device_id={"tensor": tensor_peer(d)}, device_id_type=MESH
        )

    pl.semaphore_wait(barrier, parts + peers - 2)

    up = ((y + 1) % ring) * 2 + xh
    down = ((y + ring - 1) % ring) * 2 + xh
    across = y * 2 + 1 - xh

    def slot(k, column):
        side = xh if column == 0 else 1 - xh
        return ((y + ring - k) % ring) * 2 + side

    def x_copy(index, source, at, target):
        return pltpu.make_async_remote_copy(
            src_ref=source,
            dst_ref=xg.at[at],
            send_sem=x_send.at[index],
            recv_sem=x_recv.at[at],
            device_id={"tensor": target},
            device_id_type=MESH,
        )

    half = own // 2
    own_half = pl.ds(pl.multiple_of(core * half, half), half)
    other_half = pl.ds(pl.multiple_of((1 - core) * half, half), half)

    def w_copy(index, source, at, target):
        return pltpu.make_async_remote_copy(
            src_ref=source,
            dst_ref=woutg.at[at, own_half],
            send_sem=w_send.at[index],
            recv_sem=w_recv.at[at],
            device_id={"tensor": target},
            device_id_type=MESH,
        )

    def c_copy(at, part):
        return pltpu.make_async_remote_copy(
            src_ref=woutg.at[at, part],
            dst_ref=woutg.at[at, part],
            send_sem=c_send.at[at],
            recv_sem=c_recv.at[at],
            device_id={"nodes": other_core},
            device_id_type=MESH,
        )

    def ring_stages(make, first, gathered, arrived):
        sent = []

        def send(source, at, target):
            copy = make(len(sent), source, at, target)
            copy.start()
            sent.append(copy)

        def wait(at):
            make(0, gathered(at), at, up).wait_recv()

        send(first, t, up)
        send(first, t, down)
        send(first, t, across)
        yield
        s = slot(0, 1)
        wait(s)
        send(gathered(s), s, up)
        send(gathered(s), s, down)
        arrived(s)
        yield
        last = ring // 2
        for k in range(1, last + 1):
            got = []
            for column in range(2):
                if k < last or column == 0:
                    s = slot(k, column)
                    wait(s)
                    if k < last - 1 or (k == last - 1 and column == 0):
                        send(gathered(s), s, up)
                    got.append(s)
                if k < last or column == 1:
                    s = slot(ring - k, column)
                    wait(s)
                    if k < last - 1 or (k == last - 1 and column == 1):
                        send(gathered(s), s, down)
                    got.append(s)
            for s in got:
                arrived(s)
            yield
        for copy in sent:
            copy.wait_send()

    gain = gain_ref[...]
    wide_lane = iota((own, 2 * HEAD), 1)

    def project(states, at):
        wide = states.astype(F32)
        inverse = lax.rsqrt(jnp.sum(wide * wide, axis=1, keepdims=True) / D + EPS)
        scaled = (wide * gain).astype(BF16)
        totals = lax.dot_general(scaled, win_ref[...], NT, preferred_element_type=F32) * inverse
        start = pl.multiple_of(at * own, own)
        query = totals[:, : 2 * HEAD].astype(BF16).astype(F32) * (1.0 / math.sqrt(HEAD))
        qs[pl.ds(start, own)] = jnp.where(wide_lane < HEAD, query, 0.0).astype(BF16)
        inside = pl.multiple_of(at % (BLOCK // own) * own, own)
        kvx[blocks_here + at // (BLOCK // own), pl.ds(inside, own)] = totals[:, HEAD:].astype(BF16)

    states_ring = ring_stages(
        x_copy, x_ref, lambda at: xg.at[at], lambda at: project(xg[at], at)
    )
    next(states_ring)

    src = src_ref[...]
    owner = lax.shift_right_logical(src, rows.bit_length() - 1)
    within = (src & (rows - 1)).astype(F32)
    high = jnp.floor(within * (1.0 / per))
    low = within - high * per
    owner_row = iota((parts, rows), 0)
    belongs = [owner[r : r + 1] == owner_row for r in range(ROUNDS)]
    before = jnp.where(iota((rows, rows), 0) < iota((rows, rows), 1), 1.0, 0.0).astype(BF16)
    member = jnp.concatenate([jnp.where(b, 1.0, 0.0) for b in belongs], axis=0).astype(BF16)
    counts = jnp.dot(member, before, preferred_element_type=F32)
    slot_row = iota((ROUNDS * per, rows), 0).astype(F32)
    wanted_high = jnp.zeros((parts, ROUNDS * per), F32)
    wanted_low = jnp.zeros((parts, ROUNDS * per), F32)
    for r in range(ROUNDS):
        rank = jnp.sum(
            jnp.where(belongs[r], counts[r * parts : (r + 1) * parts], 0.0), axis=0, keepdims=True
        )
        position = owner[r : r + 1].astype(F32) * per + rank
        for c in range(rows // 128):
            posr[r * (rows // 128) + c] = position[:, c * 128 : (c + 1) * 128]
        chosen = jnp.where(slot_row == rank + r * per, 1.0, 0.0).astype(BF16)
        wanted_high += lax.dot_general(
            jnp.where(belongs[r], high[r : r + 1], 0.0).astype(BF16),
            chosen,
            NT,
            preferred_element_type=F32,
        )
        wanted_low += lax.dot_general(
            jnp.where(belongs[r], low[r : r + 1], 0.0).astype(BF16),
            chosen,
            NT,
            preferred_element_type=F32,
        )
    wanted = wanted_high * per + wanted_low
    for o in range(parts):
        reqs[o] = wanted[o : o + 1]

    def r_copy(peer, at):
        return pltpu.make_async_remote_copy(
            src_ref=reqs.at[peer],
            dst_ref=reqr.at[at],
            send_sem=r_send.at[peer],
            recv_sem=r_recv.at[at],
            device_id={"nodes": peer},
            device_id_type=MESH,
        )

    @pl.loop(1, parts)
    def _(d):
        r_copy(node_peer(d), p).start()

    reqr[p] = reqs[p]

    diagonal = iota((128, 128), 0) == iota((128, 128), 1)
    lane_index = iota((128, rows), 1).astype(F32)

    def one_hot(row):
        column = jnp.sum(jnp.where(diagonal, row, 0.0), axis=1, keepdims=True)
        return jnp.where(lane_index == column, 1.0, 0.0).astype(BF16)

    project(x_ref[...], t)
    next(states_ring)
    next(states_ring)

    @pl.loop(1, parts)
    def _(d):
        r_copy(node_peer(d), node_peer(d)).wait_recv()

    @pl.loop(0, parts)
    def _(i):
        pick[i] = one_hot(reqr[i])

    next(states_ring)

    @pl.loop(0, parts)
    def _(i):
        place[i] = one_hot(posr[i])

    for _ in states_ring:
        pass

    following, preceding = node_peer(1), node_peer(parts - 1)
    mine = kvx.at[pl.ds(blocks_here, blocks_here)]

    def n_copy(which, target):
        return pltpu.make_async_remote_copy(
            src_ref=mine,
            dst_ref=kvx.at[pl.ds(2 * blocks_here * which, blocks_here)],
            send_sem=n_send.at[which],
            recv_sem=n_recv.at[which],
            device_id={"nodes": target},
            device_id_type=MESH,
        )

    neighbours = [n_copy(0, following), n_copy(1, preceding)]
    for copy in neighbours:
        copy.start()

    woutg[t] = wout_ref[...]
    weight_ring = ring_stages(
        w_copy,
        wout_ref.at[own_half],
        lambda at: woutg.at[at, own_half],
        lambda at: c_copy(at, own_half).start(),
    )
    next(weight_ring)

    def e_copy(peer, at):
        return pltpu.make_async_remote_copy(
            src_ref=snd.at[peer],
            dst_ref=rcv.at[:, at],
            send_sem=e_send.at[peer],
            recv_sem=e_recv.at[at],
            device_id={"nodes": peer},
            device_id_type=MESH,
        )

    def picked(i):
        table = kvx[blocks_here : 2 * blocks_here].reshape(rows, 2 * HEAD)
        got = jnp.dot(pick[i], table, preferred_element_type=F32)
        return got.astype(BF16).reshape(ROUNDS, per, 2 * HEAD)

    @pl.loop(1, parts)
    def _(d):
        peer = node_peer(d)
        snd[peer] = picked(peer)
        e_copy(peer, p).start()

    rcv[:, p] = picked(p)

    next(weight_ring)
    for copy in neighbours:
        copy.wait_recv()

    for b in range(blocks_here):
        span = slice(b * BLOCK, (b + 1) * BLOCK)
        query = qs[span]
        scores = []
        keys = []
        for j in range(NEIGH):
            at = blocks_ref[b, j] - p * blocks_here + blocks_here
            at = jnp.minimum(jnp.maximum(at, 0), 3 * blocks_here - 1)
            block = kvx[at]
            keys.append(block)
            scores.append(lax.dot_general(query, block, NT, preferred_element_type=F32))
        top = functools.reduce(jnp.maximum, scores)
        top = jnp.max(top, axis=1, keepdims=True)
        total = jnp.zeros((BLOCK, 1), F32)
        blended = jnp.zeros((BLOCK, 2 * HEAD), F32)
        for j in range(NEIGH):
            weights = jnp.exp(scores[j] - top)
            total += jnp.sum(weights, axis=1, keepdims=True)
            blended += jnp.dot(weights.astype(BF16), keys[j], preferred_element_type=F32)
        oloc[span] = blended
        mloc[span] = jnp.broadcast_to(top, (BLOCK, 2 * HEAD))
        lloc[span] = jnp.broadcast_to(total, (BLOCK, 2 * HEAD))
        next(weight_ring, None)
    for _ in weight_ring:
        pass

    @pl.loop(1, parts)
    def _(d):
        peer = node_peer(d)
        e_copy(peer, peer).wait_recv()

    chunks = rows // 128
    for r in range(ROUNDS):
        table = rcv[r].reshape(rows, 2 * HEAD)

        @pl.loop(0, chunks)
        def _(c):
            got = jnp.dot(place[r * chunks + c], table, preferred_element_type=F32)
            far[r, pl.ds(pl.multiple_of(c * 128, 128), 128)] = got

    for b in range(blocks_here):
        span = slice(b * BLOCK, (b + 1) * BLOCK)
        query = qs[span].astype(F32)
        top = mloc[span]
        edges = []
        for r in range(ROUNDS):
            score = jnp.sum(query * far[r, span], axis=1, keepdims=True) + bias_ref[r, 0]
            edges.append(jnp.broadcast_to(score, (BLOCK, 2 * HEAD)))
        new_top = functools.reduce(jnp.maximum, edges, top)
        keep = jnp.exp(top - new_top)
        total = lloc[span] * keep
        blended = oloc[span] * keep
        for r in range(ROUNDS):
            weight = jnp.exp(edges[r] - new_top)
            total += weight
            blended += weight.astype(BF16).astype(F32) * far[r, span]
        att[span] = blended / total

    def a_copy(peer, at):
        return pltpu.make_async_remote_copy(
            src_ref=atts.at[peer],
            dst_ref=attr.at[at],
            send_sem=a_send.at[peer],
            recv_sem=a_recv.at[at],
            device_id={"tensor": peer},
            device_id_type=MESH,
        )

    left = iota((half, 2 * HEAD), 1) < HEAD

    def packed(peer):
        block = att[pl.ds(pl.multiple_of(peer * own, own), own)]
        return jnp.where(left, pltpu.roll(block[:half], HEAD, 1), block[half:]).astype(BF16)

    @pl.loop(1, peers)
    def _(d):
        peer = tensor_peer(d)
        atts[peer] = packed(peer)
        a_copy(peer, t).start()

    attr[t] = packed(t)

    @pl.loop(1, peers)
    def _(d):
        c_copy(tensor_peer(d), other_half).wait_recv()

    @pl.loop(1, peers)
    def _(d):
        peer = tensor_peer(d)
        a_copy(peer, peer).wait_recv()

    tops, bottoms = [], []
    for pair in range(peers // 2):
        even = attr[2 * pair].astype(F32)
        odd = attr[2 * pair + 1].astype(F32)
        tops.append(jnp.where(left, even, pltpu.roll(odd, HEAD, 1)).astype(BF16))
        bottoms.append(jnp.where(left, pltpu.roll(even, HEAD, 1), odd).astype(BF16))
    attended = jnp.concatenate(
        [jnp.concatenate(tops, axis=1), jnp.concatenate(bottoms, axis=1)], axis=0
    )
    result = jnp.dot(attended, woutg[...].reshape(peers * own, D), preferred_element_type=F32)
    out_ref[...] = (x_ref[...].astype(F32) + result).astype(BF16)

    @pl.loop(1, parts)
    def _(d):
        peer = node_peer(d)
        r_copy(peer, p).wait_send()
        e_copy(peer, p).wait_send()

    @pl.loop(1, peers)
    def _(d):
        peer = tensor_peer(d)
        a_copy(peer, t).wait_send()
        c_copy(peer, own_half).wait_send()

    for copy in neighbours:
        copy.wait_send()


def per_device(
    node_states,
    norm_gain,
    input_weight,
    output_weight,
    expander_bias,
    local_blocks,
    expander_source,
):
    parts = lax.axis_size("nodes")
    peers = lax.axis_size("tensor")
    own = node_states.shape[0]
    rows = own * peers
    per = rows // parts
    chunks = rows // 128
    wide = 2 * HEAD
    vmem = pl.BlockSpec(memory_space=pltpu.VMEM)
    smem = pl.BlockSpec(memory_space=pltpu.SMEM)
    dma = pltpu.SemaphoreType.DMA
    return pl.pallas_call(
        functools.partial(kernel, parts, peers),
        out_shape=jax.ShapeDtypeStruct((own, D), BF16),
        in_specs=[vmem, vmem, vmem, vmem, smem, smem, vmem],
        out_specs=vmem,
        scratch_shapes=[
            pltpu.VMEM((peers, own, D), BF16),
            pltpu.VMEM((3 * rows // BLOCK, BLOCK, wide), BF16),
            pltpu.VMEM((rows, wide), BF16),
            pltpu.VMEM((parts, 1, ROUNDS * per), F32),
            pltpu.VMEM((parts, 1, ROUNDS * per), F32),
            pltpu.VMEM((ROUNDS * chunks, 1, 128), F32),
            pltpu.VMEM((parts, ROUNDS * per, rows), BF16),
            pltpu.VMEM((ROUNDS * chunks, 128, rows), BF16),
            pltpu.VMEM((parts, ROUNDS, per, wide), BF16),
            pltpu.VMEM((ROUNDS, parts, per, wide), BF16),
            pltpu.VMEM((ROUNDS, rows, wide), F32),
            pltpu.VMEM((rows, wide), F32),
            pltpu.VMEM((rows, wide), F32),
            pltpu.VMEM((rows, wide), F32),
            pltpu.VMEM((rows, wide), F32),
            pltpu.VMEM((peers, own // 2, wide), BF16),
            pltpu.VMEM((peers, own // 2, wide), BF16),
            pltpu.VMEM((peers, own, D), BF16),
            dma((peers,)),
            dma((peers,)),
            dma((peers,)),
            dma((peers,)),
            dma((peers,)),
            dma((peers,)),
            dma((parts,)),
            dma((parts,)),
            dma((parts,)),
            dma((parts,)),
            dma((2,)),
            dma((2,)),
            dma((peers,)),
            dma((peers,)),
        ],
        compiler_params=pltpu.CompilerParams(
            collective_id=0, has_side_effects=True, vmem_limit_bytes=48 * 1024 * 1024
        ),
        cost_estimate=pl.CostEstimate(
            flops=2 * rows * D * 8 * HEAD, bytes_accessed=4 * own * D * 8, transcendentals=rows * rows
        ),
    )(
        node_states,
        norm_gain.reshape(1, D),
        input_weight,
        output_weight,
        expander_bias,
        local_blocks,
        expander_source,
    )


def solution(mesh):
    in_specs = (
        P(("nodes", "tensor"), None),
        P(),
        P("tensor", None),
        P("tensor", None),
        P(None, "tensor"),
        P("nodes", None),
        P(None, "nodes"),
    )
    out_specs = P(("nodes", "tensor"), None)
    return jax.shard_map(
        per_device, mesh=mesh, in_specs=in_specs, out_specs=out_specs, check_vma=False
    )
```

```python
import functools
import math

import jax
import jax.numpy as jnp
from jax import lax
from jax.experimental import pallas as pl
from jax.experimental.pallas import tpu as pltpu
from jax.sharding import PartitionSpec as P

D = 1024
HEAD = 64
BLOCK = 256
NEIGH = 4
ROUNDS = 4
EPS = 1e-05
CHUNKS = 2
GROUPS = ((0, 16), (16, 24), (24, 32))

BF16 = jnp.bfloat16
F32 = jnp.float32
I32 = jnp.int32
MESH = pl.DeviceIdType.MESH
NT = (((1,), (1,)), ((), ()))


def iota(shape, dim):
    return lax.broadcasted_iota(I32, shape, dim)


def kernel(
    parts,
    peers,
    x_ref,
    gain_ref,
    win_ref,
    wout_ref,
    bias_ref,
    blocks_ref,
    src_ref,
    out_ref,
    xown,
    gain_v,
    win_v,
    win_t,
    bias_in,
    bias_out,
    bias_v,
    blocks_in,
    blocks_out,
    blocks_v,
    blocks_s,
    src_v,
    xg,
    kvx,
    qs,
    reqs,
    reqr,
    posr,
    place,
    snd,
    rcv,
    far,
    oloc,
    mloc,
    lloc,
    att,
    atts,
    attr,
    woutg,
    l_sem,
    s_sem,
    g_sem,
    x_send,
    x_recv,
    h_send,
    h_recv,
    w_send,
    w_recv,
    c_send,
    c_recv,
    r_send,
    r_recv,
    e_send,
    e_recv,
    n_send,
    n_recv,
    a_send,
    a_recv,
):
    own = x_ref.shape[0]
    rows = own * peers
    ring = peers // 2
    per = rows // parts
    blocks_here = rows // BLOCK
    wide = 2 * HEAD
    row_chunks = rows // 128
    p = lax.axis_index("nodes")
    t = lax.axis_index("tensor")
    core = p % 2
    base = p - core
    y, xh = t // 2, t % 2
    part = base + xh
    head = 2 * y + core
    home = core == xh

    def device(nodes, tensor):
        return {"nodes": nodes, "tensor": tensor}

    def worker(partition):
        return device(partition - partition % 2 + core, y * 2 + partition % 2)

    def distance(i):
        q, a = i // 2, i % 2
        return 8 + 16 * a + (q // 2) * (1 - q % 2) - ((q + 1) // 2) * (q % 2)

    def ahead(i):
        return worker((part + distance(i)) % parts)

    def behind(i):
        return worker((part + parts - distance(i)) % parts)

    self_slot = parts - 2
    up = device(p, ((y + 1) % ring) * 2 + xh)
    down = device(p, ((y + ring - 1) % ring) * 2 + xh)
    twin = device(base + 1 - core, t)
    swap = device(base + 1 - core, y * 2 + 1 - xh)
    cross = device((base + parts // 2) % parts + 1 - core, y * 2 + 1 - xh)
    across = device((p + parts // 2) % parts, y * 2 + 1 - xh)

    x_in = pltpu.make_async_copy(x_ref, xown, l_sem.at[0])
    gain_in = pltpu.make_async_copy(gain_ref, gain_v, l_sem.at[1])
    bias_load = pltpu.make_async_copy(bias_ref, bias_in, l_sem.at[2])
    blocks_load = pltpu.make_async_copy(blocks_ref, blocks_in, l_sem.at[3])
    wout_in = pltpu.make_async_copy(wout_ref, woutg.at[t], l_sem.at[4])
    for copy in (bias_load, blocks_load, gain_in, x_in, wout_in):
        copy.start()

    def local(source, target, sem):
        return pltpu.make_async_copy(source, target, sem)

    def remote(source, target, send, recv, to):
        return pltpu.make_async_remote_copy(
            src_ref=source,
            dst_ref=target,
            send_sem=send,
            recv_sem=recv,
            device_id=to,
            device_id_type=MESH,
        )

    chunk = own // CHUNKS

    def piece(at, c):
        return xg.at[at, pl.ds(c * chunk, chunk)]

    @pl.when(home)
    def _():
        for c in range(CHUNKS):
            local(x_ref.at[pl.ds(c * chunk, chunk)], piece(t, c), x_recv.at[t, c]).start()
        local(win_ref, win_v, g_sem.at[0]).start()
        local(src_ref, src_v, g_sem.at[1]).start()

    barrier = pltpu.get_barrier_semaphore()

    def greet(to):
        pl.semaphore_signal(barrier, inc=1, device_id=to, device_id_type=MESH)

    for to in (up, down, twin, swap, cross):
        greet(to)

    @pl.loop(0, parts)
    def _(i):
        @pl.when(i != self_slot)
        def _():
            greet(ahead(i))

    bias_load.wait()
    bias_out[...] = jnp.broadcast_to(
        jnp.concatenate([bias_in[...], jnp.zeros((8 - ROUNDS, 1), F32)], axis=0), (8, 128)
    )
    blocks_load.wait()
    blocks_out[0:blocks_here, 0:NEIGH] = blocks_in[...]

    @pl.when(home)
    def _():
        bias_v[...] = bias_out[...]
        blocks_v[...] = blocks_out[...]

    pl.semaphore_wait(barrier, parts + 4)

    def swap_x(c):
        return remote(
            x_ref.at[pl.ds(c * chunk, chunk)], piece(t, c), s_sem.at[c], x_recv.at[t, c], swap
        )

    cross_w = remote(win_ref, win_v, s_sem.at[CHUNKS], g_sem.at[0], cross)
    cross_b = remote(bias_out, bias_v, s_sem.at[CHUNKS + 1], g_sem.at[2], cross)
    twin_s = remote(src_ref, src_v, s_sem.at[0], g_sem.at[1], twin)
    twin_b = remote(blocks_out, blocks_v, s_sem.at[1], g_sem.at[3], twin)

    @pl.when(jnp.logical_not(home))
    def _():
        for c in range(CHUNKS):
            swap_x(c).start()
        cross_w.start()
        cross_b.start()

    @pl.when(home)
    def _():
        twin_s.start()
        twin_b.start()

    sent = []

    def x_forward(at, c, to):
        copy = remote(piece(at, c), piece(at, c), x_send.at[len(sent)], x_recv.at[at, c], to)
        copy.start()
        sent.append(copy)

    def x_wait(at, c):
        remote(piece(at, c), piece(at, c), x_send.at[0], x_recv.at[at, c], up).wait_recv()

    def hand(at):
        return remote(xg.at[at], xg.at[at], h_send.at[at // 2], h_recv.at[at // 2], twin)

    def mate(k):
        return (y + ring + k) % ring

    first = 2 * y + core
    for c in range(CHUNKS):
        x_wait(first, c)
        x_forward(first, c, up)
        x_forward(first, c, down)
    hand(first).start()

    local(src_ref, src_v, g_sem.at[1]).wait()
    src = src_v[...]
    owner = lax.shift_right_logical(src, rows.bit_length() - 1)
    within = (src & (rows - 1)).astype(F32)
    gap = (part + parts - owner) & (parts - 1)
    offset = (gap & (parts // 2 - 1)) - parts // 4
    turn = jnp.where(offset < 0, -2 * offset - 1, 2 * offset)
    slot = 2 * turn + lax.shift_right_logical(gap, (parts // 2).bit_length() - 1)
    high = jnp.floor(within * (1.0 / per))
    low = within - high * per
    slot_rows = iota((parts, rows), 0)
    belongs = [slot[r : r + 1] == slot_rows for r in range(ROUNDS)]
    before = jnp.where(iota((rows, rows), 0) < iota((rows, rows), 1), 1.0, 0.0).astype(BF16)
    member = jnp.concatenate([jnp.where(b, 1.0, 0.0) for b in belongs], axis=0).astype(BF16)
    counts = jnp.dot(member, before, preferred_element_type=F32)
    entry = iota((ROUNDS * per, rows), 0).astype(F32)
    wanted_high = jnp.zeros((parts, ROUNDS * per), F32)
    wanted_low = jnp.zeros((parts, ROUNDS * per), F32)
    for r in range(ROUNDS):
        rank = jnp.sum(
            jnp.where(belongs[r], counts[r * parts : (r + 1) * parts], 0.0), axis=0, keepdims=True
        )
        position = slot[r : r + 1].astype(F32) * per + rank
        for c in range(row_chunks):
            posr[r * row_chunks + c] = position[:, c * 128 : (c + 1) * 128]
        chosen = jnp.where(entry == rank + r * per, 1.0, 0.0).astype(BF16)
        wanted_high += lax.dot_general(
            jnp.where(belongs[r], high[r : r + 1], 0.0).astype(BF16),
            chosen,
            NT,
            preferred_element_type=F32,
        )
        wanted_low += lax.dot_general(
            jnp.where(belongs[r], low[r : r + 1], 0.0).astype(BF16),
            chosen,
            NT,
            preferred_element_type=F32,
        )
    wanted = wanted_high * per + wanted_low
    for i in range(parts):
        reqs[i] = wanted[i : i + 1]

    def r_copy(i, to):
        return remote(reqs.at[i], reqr.at[i], r_send.at[i], r_recv.at[i], to)

    @pl.loop(0, parts)
    def _(i):
        @pl.when(i != self_slot)
        def _():
            r_copy(i, behind(i)).start()

    reqr[self_slot] = reqs[self_slot]

    local(win_ref, win_v, g_sem.at[0]).wait()
    win_t[...] = jnp.transpose(win_v[...].astype(F32)).astype(BF16)
    gain_in.wait()
    gain = gain_v[...]
    wide_lane = iota((2 * own, wide), 1)

    def project(pair):
        hand(2 * pair + 1 - core).wait_recv()
        states = xg[pl.ds(2 * pair, 2)].reshape(2 * own, D).astype(F32)
        inverse = lax.rsqrt(jnp.sum(states * states, axis=1, keepdims=True) / D + EPS)
        scaled = (states * gain).astype(BF16)
        totals = jnp.dot(scaled, win_t[...], preferred_element_type=F32) * inverse
        start = pl.multiple_of(pair * 2 * own, 2 * own)
        query = totals[:, :wide].astype(BF16).astype(F32) * (1.0 / math.sqrt(HEAD))
        qs[pl.ds(start, 2 * own)] = jnp.where(wide_lane < HEAD, query, 0.0).astype(BF16)
        pairs = BLOCK // (2 * own)
        inside = pl.multiple_of(pair % pairs * 2 * own, 2 * own)
        kvx[blocks_here + pair // pairs, pl.ds(inside, 2 * own)] = totals[:, HEAD:].astype(BF16)

    last = ring // 2
    for k in range(1, last):
        below, above = 2 * mate(-k) + core, 2 * mate(k) + core
        for c in range(CHUNKS):
            x_wait(below, c)
            if k < last - 1 or c < CHUNKS // 2:
                x_forward(below, c, up)
            x_wait(above, c)
            if k < last - 1 or c >= CHUNKS // 2:
                x_forward(above, c, down)
        hand(below).start()
        hand(above).start()
        if k == 1:
            project(y)
        else:
            project(mate(1 - k))
            project(mate(k - 1))
    opposite = 2 * mate(last) + core
    for c in range(CHUNKS):
        x_wait(opposite, c)
    hand(opposite).start()
    project(mate(1 - last))
    project(mate(last - 1))
    project(mate(last))

    mine = kvx.at[pl.ds(blocks_here, blocks_here)]
    neighbours = [
        remote(
            mine,
            kvx.at[pl.ds(2 * blocks_here * which, blocks_here)],
            n_send.at[which],
            n_recv.at[which],
            to,
        )
        for which, to in enumerate((worker((part + 1) % parts), worker((part + parts - 1) % parts)))
    ]

    half = own // 2
    own_half = pl.ds(pl.multiple_of(core * half, half), half)
    other_half = pl.ds(pl.multiple_of((1 - core) * half, half), half)
    weights_sent = []

    def w_send_to(source, at, to):
        copy = remote(
            source, woutg.at[at, own_half], w_send.at[len(weights_sent)], w_recv.at[at], to
        )
        copy.start()
        weights_sent.append(copy)

    def w_wait(at):
        part_of = woutg.at[at, own_half]
        remote(part_of, part_of, w_send.at[0], w_recv.at[at], up).wait_recv()

    def c_copy(at, side):
        part_of = woutg.at[at, side]
        return remote(part_of, part_of, c_send.at[at], c_recv.at[at], twin)

    def weight_ring():
        mine = wout_ref.at[own_half]
        for to in (up, down, across):
            w_send_to(mine, t, to)
        yield
        at = 2 * y + 1 - xh
        w_wait(at)
        for to in (up, down):
            w_send_to(woutg.at[at, own_half], at, to)
        c_copy(at, own_half).start()
        yield
        for k in range(1, last + 1):
            for column in range(2):
                side = xh if column == 0 else 1 - xh
                for way, to in ((-k, up), (k, down)):
                    turned = column == 0 if way < 0 else column == 1
                    if k == last and not turned:
                        continue
                    at = 2 * mate(way) + side
                    w_wait(at)
                    if k < last - 1 or (k == last - 1 and turned):
                        w_send_to(woutg.at[at, own_half], at, to)
                    c_copy(at, own_half).start()
            yield

    weight_steps = weight_ring()

    diagonal = iota((128, 128), 0) == iota((128, 128), 1)
    lane_index = iota((128, rows), 1).astype(F32)

    def one_hot(row):
        column = jnp.sum(jnp.where(diagonal, row, 0.0), axis=1, keepdims=True)
        return jnp.where(lane_index == column, 1.0, 0.0).astype(BF16)

    def e_copy(i, to):
        return remote(snd.at[i], rcv.at[:, i], e_send.at[i], e_recv.at[i], to)

    def picked(i):
        table = kvx[blocks_here : 2 * blocks_here].reshape(rows, wide)
        got = jnp.dot(one_hot(reqr[i]), table, preferred_element_type=F32)
        return got.astype(BF16).reshape(ROUNDS, per, wide)

    steps = 4
    for step in range(steps):

        @pl.loop(step * parts // steps, (step + 1) * parts // steps)
        def _(i):
            @pl.when(i != self_slot)
            def _():
                r_copy(i, ahead(i)).wait_recv()
                snd[i] = picked(i)
                e_copy(i, ahead(i)).start()

        if step == 0:
            for copy in neighbours:
                copy.start()
        next(weight_steps)

    rcv[:, self_slot] = picked(self_slot)

    @pl.loop(0, ROUNDS * row_chunks)
    def _(i):
        place[i] = one_hot(posr[i])

    for _ in weight_steps:
        pass

    @pl.when(jnp.logical_not(home))
    def _():
        cross_b.wait_recv()
        twin_b.wait_recv()

    blocks_copy = pltpu.make_async_copy(blocks_v, blocks_s, l_sem.at[3])
    blocks_copy.start()
    blocks_copy.wait()
    for copy in neighbours:
        copy.wait_recv()
    for b in range(blocks_here):
        span = slice(b * BLOCK, (b + 1) * BLOCK)
        query = qs[span]
        scores = []
        keys = []
        for j in range(NEIGH):
            at = blocks_s[b, j] - part * blocks_here + blocks_here
            at = jnp.minimum(jnp.maximum(at, 0), 3 * blocks_here - 1)
            block = kvx[at]
            keys.append(block)
            scores.append(lax.dot_general(query, block, NT, preferred_element_type=F32))
        top = functools.reduce(jnp.maximum, scores)
        top = jnp.max(top, axis=1, keepdims=True)
        total = jnp.zeros((BLOCK, 1), F32)
        blended = jnp.zeros((BLOCK, wide), F32)
        for j in range(NEIGH):
            weights = jnp.exp(scores[j] - top)
            total += jnp.sum(weights, axis=1, keepdims=True)
            blended += jnp.dot(weights.astype(BF16), keys[j], preferred_element_type=F32)
        oloc[span] = blended
        mloc[span] = jnp.broadcast_to(top, (BLOCK, wide))
        lloc[span] = jnp.broadcast_to(total, (BLOCK, wide))

    for group, (low_slot, high_slot) in enumerate(GROUPS):

        @pl.loop(low_slot, high_slot)
        def _(i):
            @pl.when(i != self_slot)
            def _():
                e_copy(i, behind(i)).wait_recv()

        for r in range(ROUNDS):
            table = rcv[r, low_slot:high_slot].reshape((high_slot - low_slot) * per, wide)

            @pl.loop(0, row_chunks)
            def _(c):
                chosen = place[r * row_chunks + c, :, low_slot * per : high_slot * per]
                got = jnp.dot(chosen, table, preferred_element_type=F32)
                span = pl.ds(pl.multiple_of(c * 128, 128), 128)
                if group == 0:
                    far[r, span] = got
                else:
                    far[r, span] += got

    for b in range(blocks_here):
        span = slice(b * BLOCK, (b + 1) * BLOCK)
        query = qs[span].astype(F32)
        top = mloc[span]
        edges = []
        for r in range(ROUNDS):
            score = jnp.sum(query * far[r, span], axis=1, keepdims=True)
            edges.append(jnp.broadcast_to(score, (BLOCK, wide)) + bias_v[r : r + 1])
        new_top = functools.reduce(jnp.maximum, edges, top)
        keep = jnp.exp(top - new_top)
        total = lloc[span] * keep
        blended = oloc[span] * keep
        for r in range(ROUNDS):
            weight = jnp.exp(edges[r] - new_top)
            total += weight
            blended += weight.astype(BF16).astype(F32) * far[r, span]
        att[span] = blended / total

    left = iota((half, wide), 1) < HEAD

    def packed(at):
        block = att[pl.ds(pl.multiple_of(at * own, own), own)]
        return jnp.where(left, pltpu.roll(block[:half], HEAD, 1), block[half:]).astype(BF16)

    def a_copy(source, to_at, slot_at, send):
        return remote(
            source, attr.at[slot_at], a_send.at[send], a_recv.at[slot_at], device(part, to_at)
        )

    order = [(k, s) for k in (4, 3, -3, 2, -2, 1, -1, 0) for s in (1, 0)]
    owners = [2 * mate(k) + ((xh + s) % 2) for k, s in order]
    for i, at in enumerate(owners):
        if i < len(owners) - 1:
            atts[i] = packed(at)
            a_copy(atts.at[i], at, head, i).start()
        else:
            atts[i] = packed(at)

            @pl.when(home)
            def _():
                attr[head] = atts[i]

            @pl.when(jnp.logical_not(home))
            def _():
                a_copy(atts.at[i], at, head, i).start()

    for at in range(peers):

        @pl.when(at != t)
        def _():
            c_copy(at, other_half).wait_recv()

    wout_in.wait()
    x_in.wait()
    for at in range(peers):

        @pl.when(jnp.logical_or(at != head, jnp.logical_not(home)))
        def _():
            a_copy(atts.at[0], t, at, 0).wait_recv()

    tops, bottoms = [], []
    for pair in range(peers // 2):
        even = attr[2 * pair].astype(F32)
        odd = attr[2 * pair + 1].astype(F32)
        tops.append(jnp.where(left, even, pltpu.roll(odd, HEAD, 1)).astype(BF16))
        bottoms.append(jnp.where(left, pltpu.roll(even, HEAD, 1), odd).astype(BF16))
    attended = jnp.concatenate(
        [jnp.concatenate(tops, axis=1), jnp.concatenate(bottoms, axis=1)], axis=0
    )
    result = jnp.dot(attended, woutg[...].reshape(peers * own, D), preferred_element_type=F32)
    out_ref[...] = (xown[...].astype(F32) + result).astype(BF16)

    @pl.when(jnp.logical_not(home))
    def _():
        for c in range(CHUNKS):
            swap_x(c).wait_send()
        cross_w.wait_send()
        cross_b.wait_send()
        a_copy(atts.at[peers - 1], owners[-1], head, peers - 1).wait_send()

    @pl.when(home)
    def _():
        twin_s.wait_send()
        twin_b.wait_send()

    for copy in sent + weights_sent + neighbours:
        copy.wait_send()

    @pl.loop(0, parts)
    def _(i):
        @pl.when(i != self_slot)
        def _():
            r_copy(i, behind(i)).wait_send()
            e_copy(i, ahead(i)).wait_send()

    for k in range(ring):
        hand(2 * k + core).wait_send()
    for i in range(peers - 1):
        a_copy(atts.at[i], owners[i], head, i).wait_send()
    for at in range(peers):

        @pl.when(at != t)
        def _():
            c_copy(at, own_half).wait_send()


def per_device(
    node_states,
    norm_gain,
    input_weight,
    output_weight,
    expander_bias,
    local_blocks,
    expander_source,
):
    parts = lax.axis_size("nodes")
    peers = lax.axis_size("tensor")
    own = node_states.shape[0]
    rows = own * peers
    per = rows // parts
    chunks = rows // 128
    wide = 2 * HEAD
    blocks_here = rows // BLOCK
    dma = pltpu.SemaphoreType.DMA
    vmem = pltpu.VMEM
    return pl.pallas_call(
        functools.partial(kernel, parts, peers),
        out_shape=jax.ShapeDtypeStruct((own, D), BF16),
        in_specs=[pl.BlockSpec(memory_space=pl.ANY)] * 7,
        out_specs=pl.BlockSpec(memory_space=pltpu.VMEM),
        scratch_shapes=[
            vmem((own, D), BF16),
            vmem((1, D), F32),
            vmem((3 * HEAD, D), BF16),
            vmem((D, 3 * HEAD), BF16),
            vmem((ROUNDS, 1), F32),
            vmem((8, 128), F32),
            vmem((8, 128), F32),
            vmem((blocks_here, NEIGH), I32),
            vmem((8, 128), I32),
            vmem((8, 128), I32),
            pltpu.SMEM((8, 128), I32),
            vmem((ROUNDS, rows), I32),
            vmem((peers, own, D), BF16),
            vmem((3 * blocks_here, BLOCK, wide), BF16),
            vmem((rows, wide), BF16),
            vmem((parts, 1, ROUNDS * per), F32),
            vmem((parts, 1, ROUNDS * per), F32),
            vmem((ROUNDS * chunks, 1, 128), F32),
            vmem((ROUNDS * chunks, 128, rows), BF16),
            vmem((parts, ROUNDS, per, wide), BF16),
            vmem((ROUNDS, parts, per, wide), BF16),
            vmem((ROUNDS, rows, wide), F32),
            vmem((rows, wide), F32),
            vmem((rows, wide), F32),
            vmem((rows, wide), F32),
            vmem((rows, wide), F32),
            vmem((peers, own // 2, wide), BF16),
            vmem((peers, own // 2, wide), BF16),
            vmem((peers, own, D), BF16),
            dma((5,)),
            dma((CHUNKS + 2,)),
            dma((4,)),
            dma((8 * CHUNKS,)),
            dma((peers, CHUNKS)),
            dma((peers // 2,)),
            dma((peers // 2,)),
            dma((peers,)),
            dma((peers,)),
            dma((peers,)),
            dma((peers,)),
            dma((parts,)),
            dma((parts,)),
            dma((parts,)),
            dma((parts,)),
            dma((2,)),
            dma((2,)),
            dma((peers,)),
            dma((peers,)),
        ],
        compiler_params=pltpu.CompilerParams(
            collective_id=0, has_side_effects=True, vmem_limit_bytes=40 * 1024 * 1024
        ),
        cost_estimate=pl.CostEstimate(
            flops=2 * rows * D * 8 * HEAD, bytes_accessed=4 * own * D * 8, transcendentals=rows * rows
        ),
    )(
        node_states,
        norm_gain.reshape(1, D),
        input_weight,
        output_weight,
        expander_bias,
        local_blocks,
        expander_source,
    )


def solution(mesh):
    in_specs = (
        P(("nodes", "tensor"), None),
        P(),
        P("tensor", None),
        P("tensor", None),
        P(None, "tensor"),
        P("nodes", None),
        P(None, "nodes"),
    )
    out_specs = P(("nodes", "tensor"), None)
    return jax.shard_map(
        per_device, mesh=mesh, in_specs=in_specs, out_specs=out_specs, check_vma=False
    )
```

```python
import functools
import math

import jax
import jax.numpy as jnp
from jax import lax
from jax.experimental import pallas as pl
from jax.experimental.pallas import tpu as pltpu
from jax.sharding import PartitionSpec as P

D = 1024
HEAD = 64
BLOCK = 256
NEIGH = 4
ROUNDS = 4
EPS = 1e-05
CHUNKS = 2

BF16 = jnp.bfloat16
F32 = jnp.float32
I32 = jnp.int32
MESH = pl.DeviceIdType.MESH
NT = (((1,), (1,)), ((), ()))


def iota(shape, dim):
    return lax.broadcasted_iota(I32, shape, dim)


def kernel(
    parts,
    peers,
    x_ref,
    gain_ref,
    win_ref,
    wout_ref,
    bias_ref,
    blocks_ref,
    src_ref,
    out_ref,
    xown,
    gain_v,
    win_v,
    win_t,
    bias_in,
    bias_out,
    bias_v,
    blocks_in,
    blocks_out,
    blocks_v,
    blocks_s,
    src_v,
    xg,
    kvx,
    qs,
    reqs,
    reqr,
    posr,
    place,
    snd,
    rcv,
    oloc,
    mloc,
    lloc,
    atts,
    attr,
    woutg,
    l_sem,
    s_sem,
    g_sem,
    x_send,
    x_recv,
    h_send,
    h_recv,
    w_send,
    w_recv,
    c_send,
    c_recv,
    r_send,
    r_recv,
    e_send,
    e_recv,
    n_send,
    n_recv,
    a_send,
    a_recv,
):
    own = x_ref.shape[0]
    rows = own * peers
    ring = peers // 2
    per = rows // parts
    blocks_here = rows // BLOCK
    wide = 2 * HEAD
    row_chunks = rows // 128
    p = lax.axis_index("nodes")
    t = lax.axis_index("tensor")
    core = p % 2
    base = p - core
    y, xh = t // 2, t % 2
    part = base + xh
    head = 2 * y + core
    home = core == xh

    def device(nodes, tensor):
        return {"nodes": nodes, "tensor": tensor}

    def worker(partition):
        return device(partition - partition % 2 + core, y * 2 + partition % 2)

    def distance(i):
        q, a = i // 2, i % 2
        return 8 + 16 * a + (q // 2) * (1 - q % 2) - ((q + 1) // 2) * (q % 2)

    def ahead(i):
        return worker((part + distance(i)) % parts)

    def behind(i):
        return worker((part + parts - distance(i)) % parts)

    self_slot = parts - 2
    up = device(p, ((y + 1) % ring) * 2 + xh)
    down = device(p, ((y + ring - 1) % ring) * 2 + xh)
    twin = device(base + 1 - core, t)
    swap = device(base + 1 - core, y * 2 + 1 - xh)
    swap_up = device(base + 1 - core, ((y + 1) % ring) * 2 + 1 - xh)
    swap_down = device(base + 1 - core, ((y + ring - 1) % ring) * 2 + 1 - xh)
    cross = device((base + parts // 2) % parts + 1 - core, y * 2 + 1 - xh)
    across = device((p + parts // 2) % parts, y * 2 + 1 - xh)

    x_in = pltpu.make_async_copy(x_ref, xown, l_sem.at[0])
    gain_in = pltpu.make_async_copy(gain_ref, gain_v, l_sem.at[1])
    bias_load = pltpu.make_async_copy(bias_ref, bias_in, l_sem.at[2])
    blocks_load = pltpu.make_async_copy(blocks_ref, blocks_in, l_sem.at[3])
    wout_in = pltpu.make_async_copy(wout_ref, woutg.at[t], l_sem.at[4])
    for copy in (bias_load, blocks_load, gain_in, x_in, wout_in):
        copy.start()

    def local(source, target, sem):
        return pltpu.make_async_copy(source, target, sem)

    def remote(source, target, send, recv, to):
        return pltpu.make_async_remote_copy(
            src_ref=source,
            dst_ref=target,
            send_sem=send,
            recv_sem=recv,
            device_id=to,
            device_id_type=MESH,
        )

    chunk = own // CHUNKS

    def piece(at, c):
        return xg.at[at, pl.ds(c * chunk, chunk)]

    @pl.when(home)
    def _():
        for c in range(CHUNKS):
            local(x_ref.at[pl.ds(c * chunk, chunk)], piece(t, c), x_recv.at[t, c]).start()
        local(win_ref, win_v, g_sem.at[0]).start()
        local(src_ref, src_v, g_sem.at[1]).start()

    barrier = pltpu.get_barrier_semaphore()

    def greet(to):
        pl.semaphore_signal(barrier, inc=1, device_id=to, device_id_type=MESH)

    for to in (up, down, twin, swap, swap_up, swap_down, cross):
        greet(to)

    @pl.loop(0, parts)
    def _(i):
        @pl.when(i != self_slot)
        def _():
            greet(ahead(i))

    bias_load.wait()
    for r in range(ROUNDS):
        bias_out[r : r + 1] = jnp.broadcast_to(bias_in[:, r : r + 1], (1, 128))
    blocks_load.wait()
    blocks_out[0:blocks_here, 0:NEIGH] = blocks_in[...]

    @pl.when(home)
    def _():
        bias_v[...] = bias_out[...]
        blocks_v[...] = blocks_out[...]

    pl.semaphore_wait(barrier, parts + 6)

    def swap_x(c, to):
        return remote(
            x_ref.at[pl.ds(c * chunk, chunk)],
            piece(t, c),
            s_sem.at[to * CHUNKS + c],
            x_recv.at[t, c],
            (swap, swap_up, swap_down)[to],
        )

    cross_w = remote(win_ref, win_v, s_sem.at[3 * CHUNKS], g_sem.at[0], cross)
    cross_b = remote(bias_out, bias_v, s_sem.at[3 * CHUNKS + 1], g_sem.at[2], cross)
    twin_s = remote(src_ref, src_v, s_sem.at[3 * CHUNKS], g_sem.at[1], twin)
    twin_b = remote(blocks_out, blocks_v, s_sem.at[3 * CHUNKS + 1], g_sem.at[3], twin)

    @pl.when(jnp.logical_not(home))
    def _():
        for c in range(CHUNKS):
            for to in (1, 2, 0):
                swap_x(c, to).start()
        cross_w.start()
        cross_b.start()

    @pl.when(home)
    def _():
        twin_s.start()
        twin_b.start()

    sent = []

    def x_forward(at, c, to):
        copy = remote(piece(at, c), piece(at, c), x_send.at[len(sent)], x_recv.at[at, c], to)
        copy.start()
        sent.append(copy)

    def x_wait(at, c):
        remote(piece(at, c), piece(at, c), x_send.at[0], x_recv.at[at, c], up).wait_recv()

    def hand(at):
        return remote(xg.at[at], xg.at[at], h_send.at[at // 2], h_recv.at[at // 2], twin)

    def mate(k):
        return (y + ring + k) % ring

    first = 2 * y + core

    def lead(c, to):
        start = x_ref.at[pl.ds(c * chunk, chunk)]
        return remote(
            start, piece(t, c), s_sem.at[2 * c + to], x_recv.at[t, c], (up, down)[to]
        )

    @pl.when(home)
    def _():
        for c in range(CHUNKS):
            for to in range(2):
                lead(c, to).start()

    for c in range(CHUNKS):
        x_wait(first, c)
    hand(first).start()

    local(src_ref, src_v, g_sem.at[1]).wait()
    src = src_v[...]
    owner = lax.shift_right_logical(src, rows.bit_length() - 1)
    within = (src & (rows - 1)).astype(F32)
    gap = (part + parts - owner) & (parts - 1)
    offset = (gap & (parts // 2 - 1)) - parts // 4
    turn = jnp.where(offset < 0, -2 * offset - 1, 2 * offset)
    slot = 2 * turn + lax.shift_right_logical(gap, (parts // 2).bit_length() - 1)
    high = jnp.floor(within * (1.0 / per))
    low = within - high * per
    slot_rows = iota((parts, rows), 0)
    belongs = [slot[r : r + 1] == slot_rows for r in range(ROUNDS)]
    before = jnp.where(iota((rows, rows), 0) < iota((rows, rows), 1), 1.0, 0.0).astype(BF16)
    member = jnp.concatenate([jnp.where(b, 1.0, 0.0) for b in belongs], axis=0).astype(BF16)
    counts = jnp.dot(member, before, preferred_element_type=F32)
    entry = iota((ROUNDS * per, rows), 0).astype(F32)
    wanted_high = jnp.zeros((parts, ROUNDS * per), F32)
    wanted_low = jnp.zeros((parts, ROUNDS * per), F32)
    for r in range(ROUNDS):
        rank = jnp.sum(
            jnp.where(belongs[r], counts[r * parts : (r + 1) * parts], 0.0), axis=0, keepdims=True
        )
        position = slot[r : r + 1].astype(F32) * per + rank
        for c in range(row_chunks):
            posr[r * row_chunks + c] = position[:, c * 128 : (c + 1) * 128]
        chosen = jnp.where(entry == rank + r * per, 1.0, 0.0).astype(BF16)
        wanted_high += lax.dot_general(
            jnp.where(belongs[r], high[r : r + 1], 0.0).astype(BF16),
            chosen,
            NT,
            preferred_element_type=F32,
        )
        wanted_low += lax.dot_general(
            jnp.where(belongs[r], low[r : r + 1], 0.0).astype(BF16),
            chosen,
            NT,
            preferred_element_type=F32,
        )
    wanted = wanted_high * per + wanted_low
    for i in range(parts):
        reqs[i] = wanted[i : i + 1]

    def r_copy(i, to):
        return remote(reqs.at[i], reqr.at[i], r_send.at[i], r_recv.at[i], to)

    gain_in.wait()
    wide_lane = iota((2 * own, wide), 1)
    pairs = BLOCK // (2 * own)
    neighbours = (worker((part + 1) % parts), worker((part + parts - 1) % parts))

    def n_copy(pair, which):
        inside = pl.ds(pl.multiple_of(pair % pairs * 2 * own, 2 * own), 2 * own)
        return remote(
            kvx.at[blocks_here + pair // pairs, inside],
            kvx.at[2 * blocks_here * which + pair // pairs, inside],
            n_send.at[which, pair],
            n_recv.at[which, pair],
            neighbours[which],
        )

    def project(pair):
        hand(2 * pair + 1 - core).wait_recv()
        states = xg[pl.ds(2 * pair, 2)].reshape(2 * own, D).astype(F32)
        inverse = lax.rsqrt(jnp.sum(states * states, axis=1, keepdims=True) / D + EPS)
        scaled = (states * gain_v[...]).astype(BF16)
        totals = jnp.dot(scaled, win_t[...], preferred_element_type=F32) * inverse
        start = pl.multiple_of(pair * 2 * own, 2 * own)
        query = totals[:, :wide].astype(BF16).astype(F32) * (1.0 / math.sqrt(HEAD))
        qs[pl.ds(start, 2 * own)] = jnp.where(wide_lane < HEAD, query, 0.0).astype(BF16)
        inside = pl.multiple_of(pair % pairs * 2 * own, 2 * own)
        kvx[blocks_here + pair // pairs, pl.ds(inside, 2 * own)] = totals[:, HEAD:].astype(BF16)
        for which in range(2):
            n_copy(pair, which).start()

    last = ring // 2
    for k in range(1, last):
        below, above = 2 * mate(-k) + core, 2 * mate(k) + core
        for c in range(CHUNKS):
            x_wait(below, c)
            if k < last - 1 or c < CHUNKS // 2:
                x_forward(below, c, up)
            x_wait(above, c)
            if k < last - 1 or c >= CHUNKS // 2:
                x_forward(above, c, down)
        hand(below).start()
        hand(above).start()
        if k == 1:
            @pl.loop(0, parts)
            def _(i):
                @pl.when(i != self_slot)
                def _():
                    r_copy(i, behind(i)).start()

            reqr[self_slot] = reqs[self_slot]

        elif k == 2:
            local(win_ref, win_v, g_sem.at[0]).wait()
            win_t[...] = jnp.transpose(win_v[...].astype(F32)).astype(BF16)
            project(y)
        else:
            for near in range(1, k):
                project(mate(-near))
                project(mate(near))
    opposite = 2 * mate(last) + core
    for c in range(CHUNKS):
        x_wait(opposite, c)
    hand(opposite).start()
    project(mate(1 - last))
    project(mate(last - 1))
    project(mate(last))

    half = own // 2
    own_half = pl.ds(pl.multiple_of(core * half, half), half)
    other_half = pl.ds(pl.multiple_of((1 - core) * half, half), half)
    weights_sent = []

    def w_send_to(source, at, to):
        copy = remote(
            source, woutg.at[at, own_half], w_send.at[len(weights_sent)], w_recv.at[at], to
        )
        copy.start()
        weights_sent.append(copy)

    def w_wait(at):
        part_of = woutg.at[at, own_half]
        remote(part_of, part_of, w_send.at[0], w_recv.at[at], up).wait_recv()

    def c_copy(at, side):
        part_of = woutg.at[at, side]
        return remote(part_of, part_of, c_send.at[at], c_recv.at[at], twin)

    def weight_ring():
        mine = wout_ref.at[own_half]
        for to in (up, down, across):
            w_send_to(mine, t, to)
        yield
        at = 2 * y + 1 - xh
        w_wait(at)
        for to in (up, down):
            w_send_to(woutg.at[at, own_half], at, to)
        c_copy(at, own_half).start()
        yield
        for k in range(1, last + 1):
            for column in range(2):
                side = xh if column == 0 else 1 - xh
                for way, to in ((-k, up), (k, down)):
                    turned = column == 0 if way < 0 else column == 1
                    if k == last and not turned:
                        continue
                    at = 2 * mate(way) + side
                    w_wait(at)
                    if k < last - 1 or (k == last - 1 and turned):
                        w_send_to(woutg.at[at, own_half], at, to)
                    c_copy(at, own_half).start()
            yield

    weight_steps = weight_ring()

    diagonal = iota((128, 128), 0) == iota((128, 128), 1)
    lane_index = iota((128, rows), 1).astype(F32)

    def one_hot(row):
        column = jnp.sum(jnp.where(diagonal, row, 0.0), axis=1, keepdims=True)
        return jnp.where(lane_index == column, 1.0, 0.0).astype(BF16)

    def e_copy(i, to):
        return remote(snd.at[i], rcv.at[:, i], e_send.at[i], e_recv.at[i], to)

    batch = 4

    def pick(step):
        table = kvx[blocks_here : 2 * blocks_here].reshape(rows, wide)
        chosen = [one_hot(reqr[step * batch + j]) for j in range(batch)]
        got = jnp.dot(jnp.concatenate(chosen, axis=0), table, preferred_element_type=F32)
        snd[pl.ds(step * batch, batch)] = got.astype(BF16).reshape(batch, ROUNDS, per, wide)

    def serve(step):
        for j in range(batch):
            i = step * batch + j

            @pl.when(i != self_slot)
            def _():
                r_copy(i, ahead(i)).wait_recv()

        pick(step)
        for j in range(batch):
            i = step * batch + j

            @pl.when(i != self_slot)
            def _():
                e_copy(i, ahead(i)).start()

    quarters = 4
    each = parts // batch // quarters
    for quarter in range(quarters):

        @pl.loop(quarter * each, (quarter + 1) * each)
        def _(step):
            serve(step)

        next(weight_steps)

    rcv[:, self_slot] = snd[self_slot]

    @pl.loop(0, ROUNDS * row_chunks)
    def _(i):
        span = pl.ds(pl.multiple_of(i % row_chunks * 128, 128), 128)
        place[i // row_chunks, span] = one_hot(posr[i])

    for _ in weight_steps:
        pass

    @pl.when(jnp.logical_not(home))
    def _():
        cross_b.wait_recv()
        twin_b.wait_recv()

    blocks_copy = pltpu.make_async_copy(blocks_v, blocks_s, l_sem.at[3])
    blocks_copy.start()
    blocks_copy.wait()
    for pair in range(ring):
        for which in range(2):
            n_copy(pair, which).wait_recv()
    for b in range(blocks_here):
        span = slice(b * BLOCK, (b + 1) * BLOCK)
        query = qs[span]
        scores = []
        keys = []
        for j in range(NEIGH):
            at = blocks_s[b, j] - part * blocks_here + blocks_here
            at = jnp.minimum(jnp.maximum(at, 0), 3 * blocks_here - 1)
            block = kvx[at]
            keys.append(block)
            scores.append(lax.dot_general(query, block, NT, preferred_element_type=F32))
        top = functools.reduce(jnp.maximum, scores)
        top = jnp.max(top, axis=1, keepdims=True)
        total = jnp.zeros((BLOCK, 1), F32)
        blended = jnp.zeros((BLOCK, wide), F32)
        for j in range(NEIGH):
            weights = jnp.exp(scores[j] - top)
            total += jnp.sum(weights, axis=1, keepdims=True)
            blended += jnp.dot(weights.astype(BF16), keys[j], preferred_element_type=F32)
        oloc[span] = blended
        mloc[span] = jnp.broadcast_to(top, (BLOCK, wide))
        lloc[span] = jnp.broadcast_to(total, (BLOCK, wide))

    @pl.loop(0, parts)
    def _(i):
        @pl.when(i != self_slot)
        def _():
            e_copy(i, behind(i)).wait_recv()

    left = iota((half, wide), 1) < HEAD
    share = BLOCK // own

    def a_copy(i, at):
        return remote(
            atts.at[i], attr.at[head], a_send.at[i], a_recv.at[head], device(part, at)
        )

    def a_wait(at):
        remote(atts.at[0], attr.at[at], a_send.at[0], a_recv.at[at], up).wait_recv()

    owners = []
    for turned in (2, 1, 3, 0):
        b = (t // share + turned) % blocks_here
        span = pl.ds(pl.multiple_of(b * BLOCK, BLOCK), BLOCK)
        far = [
            jnp.dot(place[r, span], rcv[r].reshape(rows, wide), preferred_element_type=F32)
            for r in range(ROUNDS)
        ]
        query = qs[span].astype(F32)
        top = mloc[span]
        edges = []
        for r in range(ROUNDS):
            score = jnp.sum(query * far[r], axis=1, keepdims=True)
            edges.append(jnp.broadcast_to(score, (BLOCK, wide)) + bias_v[r : r + 1])
        new_top = functools.reduce(jnp.maximum, edges, top)
        keep = jnp.exp(top - new_top)
        total = lloc[span] * keep
        blended = oloc[span] * keep
        for r in range(ROUNDS):
            weight = jnp.exp(edges[r] - new_top)
            total += weight
            blended += weight.astype(BF16).astype(F32) * far[r]
        attended = blended / total
        for s in range(share):
            i, at = len(owners), share * b + s
            owners.append(at)
            upper = attended[s * own : s * own + half]
            lower = attended[s * own + half : (s + 1) * own]
            atts[i] = jnp.where(left, pltpu.roll(upper, HEAD, 1), lower).astype(BF16)
            if turned:
                a_copy(i, at).start()
            else:
                here = jnp.logical_and(home, at == t)

                @pl.when(here)
                def _():
                    attr[head] = atts[i]

                @pl.when(jnp.logical_not(here))
                def _():
                    a_copy(i, at).start()

    for at in range(peers):

        @pl.when(at != t)
        def _():
            c_copy(at, other_half).wait_recv()

    wout_in.wait()
    x_in.wait()
    for at in range(peers):

        @pl.when(jnp.logical_or(at != head, jnp.logical_not(home)))
        def _():
            a_wait(at)

    tops, bottoms = [], []
    for pair in range(peers // 2):
        even = attr[2 * pair].astype(F32)
        odd = attr[2 * pair + 1].astype(F32)
        tops.append(jnp.where(left, even, pltpu.roll(odd, HEAD, 1)).astype(BF16))
        bottoms.append(jnp.where(left, pltpu.roll(even, HEAD, 1), odd).astype(BF16))
    attended = jnp.concatenate(
        [jnp.concatenate(tops, axis=1), jnp.concatenate(bottoms, axis=1)], axis=0
    )
    result = jnp.dot(attended, woutg[...].reshape(peers * own, D), preferred_element_type=F32)
    out_ref[...] = (xown[...].astype(F32) + result).astype(BF16)

    @pl.when(jnp.logical_not(home))
    def _():
        for c in range(CHUNKS):
            for to in range(3):
                swap_x(c, to).wait_send()
        cross_w.wait_send()
        cross_b.wait_send()

    @pl.when(home)
    def _():
        twin_s.wait_send()
        twin_b.wait_send()
        for c in range(CHUNKS):
            for to in range(2):
                lead(c, to).wait_send()

    for copy in sent + weights_sent:
        copy.wait_send()
    for pair in range(ring):
        for which in range(2):
            n_copy(pair, which).wait_send()

    @pl.loop(0, parts)
    def _(i):
        @pl.when(i != self_slot)
        def _():
            r_copy(i, behind(i)).wait_send()
            e_copy(i, ahead(i)).wait_send()

    for k in range(ring):
        hand(2 * k + core).wait_send()
    for i, at in enumerate(owners):

        @pl.when(jnp.logical_or(at != t, jnp.logical_not(home)))
        def _():
            a_copy(i, at).wait_send()

    for at in range(peers):

        @pl.when(at != t)
        def _():
            c_copy(at, own_half).wait_send()


def per_device(
    node_states,
    norm_gain,
    input_weight,
    output_weight,
    expander_bias,
    local_blocks,
    expander_source,
):
    parts = lax.axis_size("nodes")
    peers = lax.axis_size("tensor")
    own = node_states.shape[0]
    rows = own * peers
    per = rows // parts
    chunks = rows // 128
    wide = 2 * HEAD
    blocks_here = rows // BLOCK
    dma = pltpu.SemaphoreType.DMA
    vmem = pltpu.VMEM
    return pl.pallas_call(
        functools.partial(kernel, parts, peers),
        out_shape=jax.ShapeDtypeStruct((own, D), BF16),
        in_specs=[pl.BlockSpec(memory_space=pltpu.HBM)] * 7,
        out_specs=pl.BlockSpec(memory_space=pltpu.VMEM),
        scratch_shapes=[
            vmem((own, D), BF16),
            vmem((1, D), F32),
            vmem((3 * HEAD, D), BF16),
            vmem((D, 3 * HEAD), BF16),
            vmem((1, ROUNDS), F32),
            vmem((8, 128), F32),
            vmem((8, 128), F32),
            vmem((blocks_here, NEIGH), I32),
            vmem((8, 128), I32),
            vmem((8, 128), I32),
            pltpu.SMEM((8, 128), I32),
            vmem((ROUNDS, rows), I32),
            vmem((peers, own, D), BF16),
            vmem((3 * blocks_here, BLOCK, wide), BF16),
            vmem((rows, wide), BF16),
            vmem((parts, 1, ROUNDS * per), F32),
            vmem((parts, 1, ROUNDS * per), F32),
            vmem((ROUNDS * chunks, 1, 128), F32),
            vmem((ROUNDS, rows, rows), BF16),
            vmem((parts, ROUNDS, per, wide), BF16),
            vmem((ROUNDS, parts, per, wide), BF16),
            vmem((rows, wide), F32),
            vmem((rows, wide), F32),
            vmem((rows, wide), F32),
            vmem((peers, own // 2, wide), BF16),
            vmem((peers, own // 2, wide), BF16),
            vmem((peers, own, D), BF16),
            dma((5,)),
            dma((3 * CHUNKS + 2,)),
            dma((4,)),
            dma((8 * CHUNKS,)),
            dma((peers, CHUNKS)),
            dma((peers // 2,)),
            dma((peers // 2,)),
            dma((peers,)),
            dma((peers,)),
            dma((peers,)),
            dma((peers,)),
            dma((parts,)),
            dma((parts,)),
            dma((parts,)),
            dma((parts,)),
            dma((2, peers // 2)),
            dma((2, peers // 2)),
            dma((peers,)),
            dma((peers,)),
        ],
        compiler_params=pltpu.CompilerParams(
            collective_id=0, has_side_effects=True, vmem_limit_bytes=58 * 1024 * 1024
        ),
        cost_estimate=pl.CostEstimate(
            flops=2 * rows * D * 8 * HEAD, bytes_accessed=4 * own * D * 8, transcendentals=rows * rows
        ),
    )(
        node_states,
        norm_gain.reshape(1, D),
        input_weight,
        output_weight,
        jnp.transpose(expander_bias),
        local_blocks,
        expander_source,
    )


def solution(mesh):
    in_specs = (
        P(("nodes", "tensor"), None),
        P(),
        P("tensor", None),
        P("tensor", None),
        P(None, "tensor"),
        P("nodes", None),
        P(None, "nodes"),
    )
    out_specs = P(("nodes", "tensor"), None)
    return jax.shard_map(
        per_device, mesh=mesh, in_specs=in_specs, out_specs=out_specs, check_vma=False
    )
```

```python
import functools
import math

import jax
import jax.numpy as jnp
from jax import lax
from jax.experimental import pallas as pl
from jax.experimental.pallas import tpu as pltpu
from jax.sharding import PartitionSpec as P

D = 1024
HEAD = 64
BLOCK = 256
NEIGH = 4
ROUNDS = 4
EPS = 1e-05
CHUNKS = 2

BF16 = jnp.bfloat16
F32 = jnp.float32
I32 = jnp.int32
MESH = pl.DeviceIdType.MESH
NT = (((1,), (1,)), ((), ()))


def iota(shape, dim):
    return lax.broadcasted_iota(I32, shape, dim)


def kernel(
    parts,
    peers,
    x_ref,
    gain_ref,
    win_ref,
    wout_ref,
    bias_ref,
    blocks_ref,
    src_ref,
    out_ref,
    xown,
    gain_v,
    win_v,
    win_t,
    bias_in,
    bias_out,
    bias_v,
    blocks_in,
    blocks_out,
    blocks_v,
    blocks_s,
    src_v,
    xg,
    kvx,
    qs,
    reqs,
    reqr,
    posr,
    place,
    snd,
    rcv,
    oloc,
    mloc,
    lloc,
    atts,
    attr,
    woutg,
    l_sem,
    s_sem,
    g_sem,
    x_send,
    x_recv,
    h_send,
    h_recv,
    w_send,
    w_recv,
    c_send,
    c_recv,
    r_send,
    r_recv,
    e_send,
    e_recv,
    n_send,
    n_recv,
    a_send,
    a_recv,
    token,
    ready,
):
    own = x_ref.shape[0]
    rows = own * peers
    ring = peers // 2
    per = rows // parts
    blocks_here = rows // BLOCK
    wide = 2 * HEAD
    row_chunks = rows // 128
    p = lax.axis_index("nodes")
    t = lax.axis_index("tensor")
    core = p % 2
    base = p - core
    y, xh = t // 2, t % 2
    part = base + xh
    head = 2 * y + core
    home = core == xh

    def device(nodes, tensor):
        return {"nodes": nodes, "tensor": tensor}

    def worker(partition):
        return device(partition - partition % 2 + core, y * 2 + partition % 2)

    planes = parts // 4
    xl, z = p // (parts // 2), p // 2 % planes

    def shifted(i, plane):
        lo, hi = i % 4 // 2, i % 2
        return worker((xl + lo) % 2 * (parts // 2) + plane % planes * 2 + (xh + hi) % 2)

    def ahead(i):
        return shifted(i, z + i // 4)

    def behind(i):
        return shifted(i, z + planes - i // 4)

    self_slot = 0
    up = device(p, ((y + 1) % ring) * 2 + xh)
    down = device(p, ((y + ring - 1) % ring) * 2 + xh)
    twin = device(base + 1 - core, t)
    swap = device(base + 1 - core, y * 2 + 1 - xh)
    swap_up = device(base + 1 - core, ((y + 1) % ring) * 2 + 1 - xh)
    swap_down = device(base + 1 - core, ((y + ring - 1) % ring) * 2 + 1 - xh)
    cross = device((base + parts // 2) % parts + 1 - core, y * 2 + 1 - xh)
    across = device((p + parts // 2) % parts, y * 2 + 1 - xh)

    x_in = pltpu.make_async_copy(x_ref, xown, l_sem.at[0])
    gain_in = pltpu.make_async_copy(gain_ref, gain_v, l_sem.at[1])
    bias_load = pltpu.make_async_copy(bias_ref, bias_in, l_sem.at[2])
    blocks_load = pltpu.make_async_copy(blocks_ref, blocks_in, l_sem.at[3])
    wout_in = pltpu.make_async_copy(wout_ref, woutg.at[t], l_sem.at[4])
    for copy in (bias_load, blocks_load, gain_in, x_in, wout_in):
        copy.start()

    def local(source, target, sem):
        return pltpu.make_async_copy(source, target, sem)

    def remote(source, target, send, recv, to):
        return pltpu.make_async_remote_copy(
            src_ref=source,
            dst_ref=target,
            send_sem=send,
            recv_sem=recv,
            device_id=to,
            device_id_type=MESH,
        )

    chunk = own // CHUNKS

    def piece(at, c):
        return xg.at[at, pl.ds(c * chunk, chunk)]

    @pl.when(home)
    def _():
        for c in range(CHUNKS):
            local(x_ref.at[pl.ds(c * chunk, chunk)], piece(t, c), x_recv.at[t, c]).start()
        local(win_ref, win_v, g_sem.at[0]).start()
        local(src_ref, src_v, g_sem.at[1]).start()

    barrier = pltpu.get_barrier_semaphore()

    def greet(to):
        pl.semaphore_signal(barrier, inc=1, device_id=to, device_id_type=MESH)

    for to in (up, down, twin, swap, swap_up, swap_down, cross, ahead(1), ahead(2), ahead(3)):
        greet(to)
    higher, lower = ahead(4), behind(4)
    has_higher, has_lower = z < planes - 1, z > 0

    @pl.when(has_higher)
    def _():
        greet(higher)

    @pl.when(has_lower)
    def _():
        greet(lower)

    bias_load.wait()
    for r in range(ROUNDS):
        bias_out[r : r + 1] = jnp.broadcast_to(bias_in[:, r : r + 1], (1, 128))
    blocks_load.wait()
    blocks_out[0:blocks_here, 0:NEIGH] = blocks_in[...]

    @pl.when(home)
    def _():
        bias_v[...] = bias_out[...]
        blocks_v[...] = blocks_out[...]

    pl.semaphore_wait(barrier, 10 + jnp.minimum(z, 1) + jnp.minimum(planes - 1 - z, 1))

    def swap_x(c, to):
        return remote(
            x_ref.at[pl.ds(c * chunk, chunk)],
            piece(t, c),
            s_sem.at[to * CHUNKS + c],
            x_recv.at[t, c],
            (swap, swap_up, swap_down)[to],
        )

    cross_w = remote(win_ref, win_v, s_sem.at[3 * CHUNKS], g_sem.at[0], cross)
    cross_b = remote(bias_out, bias_v, s_sem.at[3 * CHUNKS + 1], g_sem.at[2], cross)
    twin_s = remote(src_ref, src_v, s_sem.at[3 * CHUNKS], g_sem.at[1], twin)
    twin_b = remote(blocks_out, blocks_v, s_sem.at[3 * CHUNKS + 1], g_sem.at[3], twin)

    @pl.when(jnp.logical_not(home))
    def _():
        for c in range(CHUNKS):
            for to in (1, 2, 0):
                swap_x(c, to).start()
        cross_w.start()
        cross_b.start()

    @pl.when(home)
    def _():
        twin_s.start()
        twin_b.start()

    sent = []

    def x_forward(at, c, to):
        copy = remote(piece(at, c), piece(at, c), x_send.at[len(sent)], x_recv.at[at, c], to)
        copy.start()
        sent.append(copy)

    def x_wait(at, c):
        remote(piece(at, c), piece(at, c), x_send.at[0], x_recv.at[at, c], up).wait_recv()

    def hand(at):
        return remote(xg.at[at], xg.at[at], h_send.at[at // 2], h_recv.at[at // 2], twin)

    def mate(k):
        return (y + ring + k) % ring

    first = 2 * y + core

    def lead(c, to):
        start = x_ref.at[pl.ds(c * chunk, chunk)]
        return remote(
            start, piece(t, c), s_sem.at[2 * c + to], x_recv.at[t, c], (up, down)[to]
        )

    @pl.when(home)
    def _():
        for c in range(CHUNKS):
            for to in range(2):
                lead(c, to).start()

    @pl.when(has_lower)
    def _():
        pl.semaphore_wait(token, 1)

    @pl.when(has_higher)
    def _():
        pl.semaphore_signal(token, inc=1, device_id=higher, device_id_type=MESH)

    @pl.loop(0, parts)
    def _(i):
        @pl.when(jnp.logical_and(i >= 4, i // 4 <= z))
        def _():
            pl.semaphore_signal(ready, inc=1, device_id=behind(i), device_id_type=MESH)

    for c in range(CHUNKS):
        x_wait(first, c)
    hand(first).start()

    local(src_ref, src_v, g_sem.at[1]).wait()
    src = src_v[...]
    owner = lax.shift_right_logical(src, rows.bit_length() - 1)
    within = (src & (rows - 1)).astype(F32)
    owner_plane = lax.shift_right_logical(owner, 1) & (planes - 1)
    owner_lo = lax.shift_right_logical(owner, (parts // 2).bit_length() - 1)
    slot = (
        ((z + planes - owner_plane) & (planes - 1)) * 4
        + ((owner_lo + xl) & 1) * 2
        + ((owner + xh) & 1)
    )
    high = jnp.floor(within * (1.0 / per))
    low = within - high * per
    slot_rows = iota((parts, rows), 0)
    belongs = [slot[r : r + 1] == slot_rows for r in range(ROUNDS)]
    before = jnp.where(iota((rows, rows), 0) < iota((rows, rows), 1), 1.0, 0.0).astype(BF16)
    member = jnp.concatenate([jnp.where(b, 1.0, 0.0) for b in belongs], axis=0).astype(BF16)
    counts = jnp.dot(member, before, preferred_element_type=F32)
    entry = iota((ROUNDS * per, rows), 0).astype(F32)
    wanted_high = jnp.zeros((parts, ROUNDS * per), F32)
    wanted_low = jnp.zeros((parts, ROUNDS * per), F32)
    for r in range(ROUNDS):
        rank = jnp.sum(
            jnp.where(belongs[r], counts[r * parts : (r + 1) * parts], 0.0), axis=0, keepdims=True
        )
        position = slot[r : r + 1].astype(F32) * per + rank
        for c in range(row_chunks):
            posr[r * row_chunks + c] = position[:, c * 128 : (c + 1) * 128]
        chosen = jnp.where(entry == rank + r * per, 1.0, 0.0).astype(BF16)
        wanted_high += lax.dot_general(
            jnp.where(belongs[r], high[r : r + 1], 0.0).astype(BF16),
            chosen,
            NT,
            preferred_element_type=F32,
        )
        wanted_low += lax.dot_general(
            jnp.where(belongs[r], low[r : r + 1], 0.0).astype(BF16),
            chosen,
            NT,
            preferred_element_type=F32,
        )
    wanted = wanted_high * per + wanted_low
    for i in range(parts):
        reqs[i] = wanted[i : i + 1]

    def r_copy(i, to):
        return remote(reqs.at[i], reqr.at[i], r_send.at[i], r_recv.at[i], to)

    gain_in.wait()
    wide_lane = iota((2 * own, wide), 1)
    pairs = BLOCK // (2 * own)
    neighbours = (worker((part + 1) % parts), worker((part + parts - 1) % parts))

    def n_copy(pair, which):
        inside = pl.ds(pl.multiple_of(pair % pairs * 2 * own, 2 * own), 2 * own)
        return remote(
            kvx.at[blocks_here + pair // pairs, inside],
            kvx.at[2 * blocks_here * which + pair // pairs, inside],
            n_send.at[which, pair],
            n_recv.at[which, pair],
            neighbours[which],
        )

    def project(pair):
        hand(2 * pair + 1 - core).wait_recv()
        states = xg[pl.ds(2 * pair, 2)].reshape(2 * own, D).astype(F32)
        inverse = lax.rsqrt(jnp.sum(states * states, axis=1, keepdims=True) / D + EPS)
        scaled = (states * gain_v[...]).astype(BF16)
        totals = jnp.dot(scaled, win_t[...], preferred_element_type=F32) * inverse
        start = pl.multiple_of(pair * 2 * own, 2 * own)
        query = totals[:, :wide].astype(BF16).astype(F32) * (1.0 / math.sqrt(HEAD))
        qs[pl.ds(start, 2 * own)] = jnp.where(wide_lane < HEAD, query, 0.0).astype(BF16)
        inside = pl.multiple_of(pair % pairs * 2 * own, 2 * own)
        kvx[blocks_here + pair // pairs, pl.ds(inside, 2 * own)] = totals[:, HEAD:].astype(BF16)

    def share_keys(pair):
        for which in range(2):
            n_copy(pair, which).start()

    last = ring // 2
    for k in range(1, last):
        below, above = 2 * mate(-k) + core, 2 * mate(k) + core
        for c in range(CHUNKS):
            x_wait(below, c)
            if k < last - 1 or c < CHUNKS // 2:
                x_forward(below, c, up)
            x_wait(above, c)
            if k < last - 1 or c >= CHUNKS // 2:
                x_forward(above, c, down)
        hand(below).start()
        hand(above).start()
        if k == 2:
            local(win_ref, win_v, g_sem.at[0]).wait()
            win_t[...] = jnp.transpose(win_v[...].astype(F32)).astype(BF16)
            project(y)

    @pl.when(has_higher)
    def _():
        pl.semaphore_wait(ready, (planes - 1 - z) * 4)

    @pl.loop(0, parts)
    def _(i):
        @pl.when(i != self_slot)
        def _():
            r_copy(i, behind(i)).start()

    reqr[self_slot] = reqs[self_slot]
    share_keys(y)
    for near in range(1, last - 1):
        for pair in (mate(-near), mate(near)):
            project(pair)
            share_keys(pair)
    opposite = 2 * mate(last) + core
    for c in range(CHUNKS):
        x_wait(opposite, c)
    hand(opposite).start()
    for pair in (mate(1 - last), mate(last - 1), mate(last)):
        project(pair)
        share_keys(pair)

    half = own // 2
    own_half = pl.ds(pl.multiple_of(core * half, half), half)
    other_half = pl.ds(pl.multiple_of((1 - core) * half, half), half)
    weights_sent = []

    def w_send_to(source, at, to):
        copy = remote(
            source, woutg.at[at, own_half], w_send.at[len(weights_sent)], w_recv.at[at], to
        )
        copy.start()
        weights_sent.append(copy)

    def w_wait(at):
        part_of = woutg.at[at, own_half]
        remote(part_of, part_of, w_send.at[0], w_recv.at[at], up).wait_recv()

    def c_copy(at, side):
        part_of = woutg.at[at, side]
        return remote(part_of, part_of, c_send.at[at], c_recv.at[at], twin)

    def weight_ring():
        mine = wout_ref.at[own_half]
        for to in (up, down, across):
            w_send_to(mine, t, to)
        yield
        at = 2 * y + 1 - xh
        w_wait(at)
        for to in (up, down):
            w_send_to(woutg.at[at, own_half], at, to)
        c_copy(at, own_half).start()
        yield
        for k in range(1, last + 1):
            for column in range(2):
                side = xh if column == 0 else 1 - xh
                for way, to in ((-k, up), (k, down)):
                    turned = column == 0 if way < 0 else column == 1
                    if k == last and not turned:
                        continue
                    at = 2 * mate(way) + side
                    w_wait(at)
                    if k < last - 1 or (k == last - 1 and turned):
                        w_send_to(woutg.at[at, own_half], at, to)
                    c_copy(at, own_half).start()
            yield

    weight_steps = weight_ring()

    diagonal = iota((128, 128), 0) == iota((128, 128), 1)
    lane_index = iota((128, rows), 1).astype(F32)

    def one_hot(row):
        column = jnp.sum(jnp.where(diagonal, row, 0.0), axis=1, keepdims=True)
        return jnp.where(lane_index == column, 1.0, 0.0).astype(BF16)

    def e_copy(i, to):
        return remote(snd.at[i], rcv.at[:, i], e_send.at[i], e_recv.at[i], to)

    batch = 4

    def pick(step):
        table = kvx[blocks_here : 2 * blocks_here].reshape(rows, wide)
        chosen = [one_hot(reqr[step * batch + j]) for j in range(batch)]
        got = jnp.dot(jnp.concatenate(chosen, axis=0), table, preferred_element_type=F32)
        snd[pl.ds(step * batch, batch)] = got.astype(BF16).reshape(batch, ROUNDS, per, wide)

    def serve(turn):
        farthest = planes // 2 + (turn + 1) // 2 * (1 - turn % 2 * 2)
        step = jnp.where(z < planes // 2, turn + planes - z, farthest + planes) % planes
        for j in range(batch):
            i = step * batch + j

            @pl.when(i != self_slot)
            def _():
                r_copy(i, ahead(i)).wait_recv()

        pick(step)
        for j in range(batch):
            i = step * batch + j

            @pl.when(i != self_slot)
            def _():
                e_copy(i, ahead(i)).start()

    quarters = 4
    each = planes // quarters
    for quarter in range(quarters):

        @pl.loop(quarter * each, (quarter + 1) * each)
        def _(turn):
            serve(turn)

        next(weight_steps)

    rcv[:, self_slot] = snd[self_slot]

    @pl.loop(0, ROUNDS * row_chunks)
    def _(i):
        span = pl.ds(pl.multiple_of(i % row_chunks * 128, 128), 128)
        place[i // row_chunks, span] = one_hot(posr[i])

    for _ in weight_steps:
        pass

    @pl.when(jnp.logical_not(home))
    def _():
        cross_b.wait_recv()
        twin_b.wait_recv()

    blocks_copy = pltpu.make_async_copy(blocks_v, blocks_s, l_sem.at[3])
    blocks_copy.start()
    blocks_copy.wait()
    for pair in range(ring):
        for which in range(2):
            n_copy(pair, which).wait_recv()
    for b in range(blocks_here):
        span = slice(b * BLOCK, (b + 1) * BLOCK)
        query = qs[span]
        scores = []
        keys = []
        for j in range(NEIGH):
            at = blocks_s[b, j] - part * blocks_here + blocks_here
            at = jnp.minimum(jnp.maximum(at, 0), 3 * blocks_here - 1)
            block = kvx[at]
            keys.append(block)
            scores.append(lax.dot_general(query, block, NT, preferred_element_type=F32))
        top = functools.reduce(jnp.maximum, scores)
        top = jnp.max(top, axis=1, keepdims=True)
        total = jnp.zeros((BLOCK, 1), F32)
        blended = jnp.zeros((BLOCK, wide), F32)
        for j in range(NEIGH):
            weights = jnp.exp(scores[j] - top)
            total += jnp.sum(weights, axis=1, keepdims=True)
            blended += jnp.dot(weights.astype(BF16), keys[j], preferred_element_type=F32)
        oloc[span] = blended
        mloc[span] = jnp.broadcast_to(top, (BLOCK, wide))
        lloc[span] = jnp.broadcast_to(total, (BLOCK, wide))

    @pl.loop(0, parts)
    def _(i):
        @pl.when(i != self_slot)
        def _():
            e_copy(i, behind(i)).wait_recv()

    left = iota((half, wide), 1) < HEAD
    share = BLOCK // own

    def a_copy(i, at):
        return remote(
            atts.at[i], attr.at[head], a_send.at[i], a_recv.at[head], device(part, at)
        )

    def a_wait(at):
        remote(atts.at[0], attr.at[at], a_send.at[0], a_recv.at[at], up).wait_recv()

    owners = []
    for turned in (2, 1, 3, 0):
        b = (t // share + turned) % blocks_here
        span = pl.ds(pl.multiple_of(b * BLOCK, BLOCK), BLOCK)
        far = [
            jnp.dot(place[r, span], rcv[r].reshape(rows, wide), preferred_element_type=F32)
            for r in range(ROUNDS)
        ]
        query = qs[span].astype(F32)
        top = mloc[span]
        edges = []
        for r in range(ROUNDS):
            score = jnp.sum(query * far[r], axis=1, keepdims=True)
            edges.append(jnp.broadcast_to(score, (BLOCK, wide)) + bias_v[r : r + 1])
        new_top = functools.reduce(jnp.maximum, edges, top)
        keep = jnp.exp(top - new_top)
        total = lloc[span] * keep
        blended = oloc[span] * keep
        for r in range(ROUNDS):
            weight = jnp.exp(edges[r] - new_top)
            total += weight
            blended += weight.astype(BF16).astype(F32) * far[r]
        attended = blended / total
        for s in range(share):
            i, at = len(owners), share * b + s
            owners.append(at)
            upper = attended[s * own : s * own + half]
            lower = attended[s * own + half : (s + 1) * own]
            atts[i] = jnp.where(left, pltpu.roll(upper, HEAD, 1), lower).astype(BF16)
            if turned:
                a_copy(i, at).start()
            else:
                here = jnp.logical_and(home, at == t)

                @pl.when(here)
                def _():
                    attr[head] = atts[i]

                @pl.when(jnp.logical_not(here))
                def _():
                    a_copy(i, at).start()

    for at in range(peers):

        @pl.when(at != t)
        def _():
            c_copy(at, other_half).wait_recv()

    wout_in.wait()
    x_in.wait()
    for at in range(peers):

        @pl.when(jnp.logical_or(at != head, jnp.logical_not(home)))
        def _():
            a_wait(at)

    tops, bottoms = [], []
    for pair in range(peers // 2):
        even = attr[2 * pair].astype(F32)
        odd = attr[2 * pair + 1].astype(F32)
        tops.append(jnp.where(left, even, pltpu.roll(odd, HEAD, 1)).astype(BF16))
        bottoms.append(jnp.where(left, pltpu.roll(even, HEAD, 1), odd).astype(BF16))
    attended = jnp.concatenate(
        [jnp.concatenate(tops, axis=1), jnp.concatenate(bottoms, axis=1)], axis=0
    )
    result = jnp.dot(attended, woutg[...].reshape(peers * own, D), preferred_element_type=F32)
    out_ref[...] = (xown[...].astype(F32) + result).astype(BF16)

    @pl.when(jnp.logical_not(home))
    def _():
        for c in range(CHUNKS):
            for to in range(3):
                swap_x(c, to).wait_send()
        cross_w.wait_send()
        cross_b.wait_send()

    @pl.when(home)
    def _():
        twin_s.wait_send()
        twin_b.wait_send()
        for c in range(CHUNKS):
            for to in range(2):
                lead(c, to).wait_send()

    for copy in sent + weights_sent:
        copy.wait_send()
    for pair in range(ring):
        for which in range(2):
            n_copy(pair, which).wait_send()

    @pl.loop(0, parts)
    def _(i):
        @pl.when(i != self_slot)
        def _():
            r_copy(i, behind(i)).wait_send()
            e_copy(i, ahead(i)).wait_send()

    for k in range(ring):
        hand(2 * k + core).wait_send()
    for i, at in enumerate(owners):

        @pl.when(jnp.logical_or(at != t, jnp.logical_not(home)))
        def _():
            a_copy(i, at).wait_send()

    for at in range(peers):

        @pl.when(at != t)
        def _():
            c_copy(at, own_half).wait_send()


def per_device(
    node_states,
    norm_gain,
    input_weight,
    output_weight,
    expander_bias,
    local_blocks,
    expander_source,
):
    parts = lax.axis_size("nodes")
    peers = lax.axis_size("tensor")
    own = node_states.shape[0]
    rows = own * peers
    per = rows // parts
    chunks = rows // 128
    wide = 2 * HEAD
    blocks_here = rows // BLOCK
    dma = pltpu.SemaphoreType.DMA
    vmem = pltpu.VMEM
    return pl.pallas_call(
        functools.partial(kernel, parts, peers),
        out_shape=jax.ShapeDtypeStruct((own, D), BF16),
        in_specs=[pl.BlockSpec(memory_space=pltpu.HBM)] * 7,
        out_specs=pl.BlockSpec(memory_space=pltpu.VMEM),
        scratch_shapes=[
            vmem((own, D), BF16),
            vmem((1, D), F32),
            vmem((3 * HEAD, D), BF16),
            vmem((D, 3 * HEAD), BF16),
            vmem((1, ROUNDS), F32),
            vmem((8, 128), F32),
            vmem((8, 128), F32),
            vmem((blocks_here, NEIGH), I32),
            vmem((8, 128), I32),
            vmem((8, 128), I32),
            pltpu.SMEM((8, 128), I32),
            vmem((ROUNDS, rows), I32),
            vmem((peers, own, D), BF16),
            vmem((3 * blocks_here, BLOCK, wide), BF16),
            vmem((rows, wide), BF16),
            vmem((parts, 1, ROUNDS * per), F32),
            vmem((parts, 1, ROUNDS * per), F32),
            vmem((ROUNDS * chunks, 1, 128), F32),
            vmem((ROUNDS, rows, rows), BF16),
            vmem((parts, ROUNDS, per, wide), BF16),
            vmem((ROUNDS, parts, per, wide), BF16),
            vmem((rows, wide), F32),
            vmem((rows, wide), F32),
            vmem((rows, wide), F32),
            vmem((peers, own // 2, wide), BF16),
            vmem((peers, own // 2, wide), BF16),
            vmem((peers, own, D), BF16),
            dma((5,)),
            dma((3 * CHUNKS + 2,)),
            dma((4,)),
            dma((8 * CHUNKS,)),
            dma((peers, CHUNKS)),
            dma((peers // 2,)),
            dma((peers // 2,)),
            dma((peers,)),
            dma((peers,)),
            dma((peers,)),
            dma((peers,)),
            dma((parts,)),
            dma((parts,)),
            dma((parts,)),
            dma((parts,)),
            dma((2, peers // 2)),
            dma((2, peers // 2)),
            dma((peers,)),
            dma((peers,)),
            pltpu.SemaphoreType.REGULAR,
            pltpu.SemaphoreType.REGULAR,
        ],
        compiler_params=pltpu.CompilerParams(
            collective_id=0, has_side_effects=True, vmem_limit_bytes=58 * 1024 * 1024
        ),
        cost_estimate=pl.CostEstimate(
            flops=2 * rows * D * 8 * HEAD, bytes_accessed=4 * own * D * 8, transcendentals=rows * rows
        ),
    )(
        node_states,
        norm_gain.reshape(1, D),
        input_weight,
        output_weight,
        jnp.transpose(expander_bias),
        local_blocks,
        expander_source,
    )


def solution(mesh):
    in_specs = (
        P(("nodes", "tensor"), None),
        P(),
        P("tensor", None),
        P("tensor", None),
        P(None, "tensor"),
        P("nodes", None),
        P(None, "nodes"),
    )
    out_specs = P(("nodes", "tensor"), None)
    return jax.shard_map(
        per_device, mesh=mesh, in_specs=in_specs, out_specs=out_specs, check_vma=False
    )
```

```python
import functools
import math

import jax
import jax.numpy as jnp
from jax import lax
from jax.experimental import pallas as pl
from jax.experimental.pallas import tpu as pltpu
from jax.sharding import PartitionSpec as P

D = 1024
HEAD = 64
BLOCK = 256
NEIGH = 4
ROUNDS = 4
EPS = 1e-05
CHUNKS = 2

BF16 = jnp.bfloat16
F32 = jnp.float32
I32 = jnp.int32
MESH = pl.DeviceIdType.MESH
NT = (((1,), (1,)), ((), ()))


def iota(shape, dim):
    return lax.broadcasted_iota(I32, shape, dim)


def kernel(
    parts,
    peers,
    x_ref,
    gain_ref,
    win_ref,
    wout_ref,
    bias_ref,
    blocks_ref,
    src_ref,
    out_ref,
    xown,
    gain_v,
    win_v,
    win_t,
    bias_in,
    bias_out,
    bias_v,
    blocks_in,
    blocks_out,
    blocks_v,
    blocks_s,
    src_v,
    xg,
    kvx,
    qs,
    reqs,
    reqr,
    posr,
    place,
    snd,
    rcv,
    oloc,
    mloc,
    lloc,
    atts,
    attr,
    woutg,
    l_sem,
    s_sem,
    g_sem,
    x_send,
    x_recv,
    h_send,
    h_recv,
    w_send,
    w_recv,
    c_send,
    c_recv,
    r_send,
    r_recv,
    e_send,
    e_recv,
    n_send,
    n_recv,
    a_send,
    a_recv,
    token,
    ready,
):
    own = x_ref.shape[0]
    rows = own * peers
    ring = peers // 2
    per = rows // parts
    blocks_here = rows // BLOCK
    wide = 2 * HEAD
    row_chunks = rows // 128
    p = lax.axis_index("nodes")
    t = lax.axis_index("tensor")
    core = p % 2
    base = p - core
    y, xh = t // 2, t % 2
    part = base + xh
    head = 2 * y + core
    home = core == xh

    def device(nodes, tensor):
        return {"nodes": nodes, "tensor": tensor}

    def worker(partition):
        return device(partition - partition % 2 + core, y * 2 + partition % 2)

    planes = parts // 4
    xl, z = p // (parts // 2), p // 2 % planes

    def shifted(i, plane):
        lo, hi = i % 4 // 2, i % 2
        return worker((xl + lo) % 2 * (parts // 2) + plane % planes * 2 + (xh + hi) % 2)

    def ahead(i):
        return shifted(i, z + i // 4)

    def behind(i):
        return shifted(i, z + planes - i // 4)

    self_slot = 0
    up = device(p, ((y + 1) % ring) * 2 + xh)
    down = device(p, ((y + ring - 1) % ring) * 2 + xh)
    twin = device(base + 1 - core, t)
    swap = device(base + 1 - core, y * 2 + 1 - xh)
    swap_up = device(base + 1 - core, ((y + 1) % ring) * 2 + 1 - xh)
    swap_down = device(base + 1 - core, ((y + ring - 1) % ring) * 2 + 1 - xh)
    cross = device((base + parts // 2) % parts + 1 - core, y * 2 + 1 - xh)
    across = device((p + parts // 2) % parts, y * 2 + 1 - xh)

    x_in = pltpu.make_async_copy(x_ref, xown, l_sem.at[0])
    gain_in = pltpu.make_async_copy(gain_ref, gain_v, l_sem.at[1])
    bias_load = pltpu.make_async_copy(bias_ref, bias_in, l_sem.at[2])
    blocks_load = pltpu.make_async_copy(blocks_ref, blocks_in, l_sem.at[3])
    wout_in = pltpu.make_async_copy(wout_ref, woutg.at[t], l_sem.at[4])
    for copy in (bias_load, blocks_load, gain_in, x_in, wout_in):
        copy.start()

    def local(source, target, sem):
        return pltpu.make_async_copy(source, target, sem)

    def remote(source, target, send, recv, to):
        return pltpu.make_async_remote_copy(
            src_ref=source,
            dst_ref=target,
            send_sem=send,
            recv_sem=recv,
            device_id=to,
            device_id_type=MESH,
        )

    chunk = own // CHUNKS

    def piece(at, c):
        return xg.at[at, pl.ds(c * chunk, chunk)]

    @pl.when(home)
    def _():
        for c in range(CHUNKS):
            local(x_ref.at[pl.ds(c * chunk, chunk)], piece(t, c), x_recv.at[t, c]).start()
        local(win_ref, win_v, g_sem.at[0]).start()
        local(src_ref, src_v, g_sem.at[1]).start()

    barrier = pltpu.get_barrier_semaphore()

    def greet(to):
        pl.semaphore_signal(barrier, inc=1, device_id=to, device_id_type=MESH)

    for to in (up, down, twin, swap, swap_up, swap_down, cross, ahead(1), ahead(2), ahead(3)):
        greet(to)
    higher, lower = ahead(4), behind(4)
    has_higher, has_lower = z < planes - 1, z > 0

    @pl.when(has_higher)
    def _():
        greet(higher)

    @pl.when(has_lower)
    def _():
        greet(lower)

    bias_load.wait()
    for r in range(ROUNDS):
        bias_out[r : r + 1] = jnp.broadcast_to(bias_in[:, r : r + 1], (1, 128))
    blocks_load.wait()
    blocks_out[0:blocks_here, 0:NEIGH] = blocks_in[...]

    @pl.when(home)
    def _():
        bias_v[...] = bias_out[...]
        blocks_v[...] = blocks_out[...]

    pl.semaphore_wait(barrier, 10 + jnp.minimum(z, 1) + jnp.minimum(planes - 1 - z, 1))

    def swap_x(c, to):
        return remote(
            x_ref.at[pl.ds(c * chunk, chunk)],
            piece(t, c),
            s_sem.at[to * CHUNKS + c],
            x_recv.at[t, c],
            (swap, swap_up, swap_down)[to],
        )

    cross_w = remote(win_ref, win_v, s_sem.at[3 * CHUNKS], g_sem.at[0], cross)
    cross_b = remote(bias_out, bias_v, s_sem.at[3 * CHUNKS + 1], g_sem.at[2], cross)
    twin_s = remote(src_ref, src_v, s_sem.at[3 * CHUNKS], g_sem.at[1], twin)
    twin_b = remote(blocks_out, blocks_v, s_sem.at[3 * CHUNKS + 1], g_sem.at[3], twin)

    @pl.when(jnp.logical_not(home))
    def _():
        for c in range(CHUNKS):
            for to in (1, 2, 0):
                swap_x(c, to).start()
        cross_w.start()
        cross_b.start()

    @pl.when(home)
    def _():
        twin_s.start()
        twin_b.start()

    sent = []

    def x_forward(at, c, to):
        copy = remote(piece(at, c), piece(at, c), x_send.at[len(sent)], x_recv.at[at, c], to)
        copy.start()
        sent.append(copy)

    def x_wait(at, c):
        remote(piece(at, c), piece(at, c), x_send.at[0], x_recv.at[at, c], up).wait_recv()

    def hand(at):
        return remote(xg.at[at], xg.at[at], h_send.at[at // 2], h_recv.at[at // 2], twin)

    def mate(k):
        return (y + ring + k) % ring

    first = 2 * y + core

    def lead(c, to):
        start = x_ref.at[pl.ds(c * chunk, chunk)]
        return remote(
            start, piece(t, c), s_sem.at[2 * c + to], x_recv.at[t, c], (up, down)[to]
        )

    @pl.when(home)
    def _():
        for c in range(CHUNKS):
            for to in range(2):
                lead(c, to).start()

    @pl.when(has_lower)
    def _():
        pl.semaphore_wait(token, 1)

    @pl.when(has_higher)
    def _():
        pl.semaphore_signal(token, inc=1, device_id=higher, device_id_type=MESH)

    @pl.loop(0, parts)
    def _(i):
        @pl.when(jnp.logical_and(i >= 4, i // 4 <= z))
        def _():
            pl.semaphore_signal(ready, inc=1, device_id=behind(i), device_id_type=MESH)

    for c in range(CHUNKS):
        x_wait(first, c)
    hand(first).start()

    local(src_ref, src_v, g_sem.at[1]).wait()
    src = src_v[...]
    owner = lax.shift_right_logical(src, rows.bit_length() - 1)
    within = (src & (rows - 1)).astype(F32)
    owner_plane = lax.shift_right_logical(owner, 1) & (planes - 1)
    owner_lo = lax.shift_right_logical(owner, (parts // 2).bit_length() - 1)
    slot = (
        ((z + planes - owner_plane) & (planes - 1)) * 4
        + ((owner_lo + xl) & 1) * 2
        + ((owner + xh) & 1)
    )
    high = jnp.floor(within * (1.0 / per))
    low = within - high * per
    slot_rows = iota((parts, rows), 0)
    belongs = [slot[r : r + 1] == slot_rows for r in range(ROUNDS)]
    before = jnp.where(iota((rows, rows), 0) < iota((rows, rows), 1), 1.0, 0.0).astype(BF16)
    member = jnp.concatenate([jnp.where(b, 1.0, 0.0) for b in belongs], axis=0).astype(BF16)
    counts = jnp.dot(member, before, preferred_element_type=F32)
    entry = iota((ROUNDS * per, rows), 0).astype(F32)
    wanted_high = jnp.zeros((parts, ROUNDS * per), F32)
    wanted_low = jnp.zeros((parts, ROUNDS * per), F32)
    for r in range(ROUNDS):
        rank = jnp.sum(
            jnp.where(belongs[r], counts[r * parts : (r + 1) * parts], 0.0), axis=0, keepdims=True
        )
        position = slot[r : r + 1].astype(F32) * per + rank
        for c in range(row_chunks):
            posr[r * row_chunks + c] = position[:, c * 128 : (c + 1) * 128]
        chosen = jnp.where(entry == rank + r * per, 1.0, 0.0).astype(BF16)
        wanted_high += lax.dot_general(
            jnp.where(belongs[r], high[r : r + 1], 0.0).astype(BF16),
            chosen,
            NT,
            preferred_element_type=F32,
        )
        wanted_low += lax.dot_general(
            jnp.where(belongs[r], low[r : r + 1], 0.0).astype(BF16),
            chosen,
            NT,
            preferred_element_type=F32,
        )
    wanted = wanted_high * per + wanted_low
    for i in range(parts):
        reqs[i] = wanted[i : i + 1]

    def r_copy(i, to):
        return remote(reqs.at[i], reqr.at[i], r_send.at[i], r_recv.at[i], to)

    gain_in.wait()
    wide_lane = iota((2 * own, wide), 1)
    pairs = BLOCK // (2 * own)
    neighbours = (worker((part + 1) % parts), worker((part + parts - 1) % parts))

    def n_copy(pair, which):
        inside = pl.ds(pl.multiple_of(pair % pairs * 2 * own, 2 * own), 2 * own)
        return remote(
            kvx.at[blocks_here + pair // pairs, inside],
            kvx.at[2 * blocks_here * which + pair // pairs, inside],
            n_send.at[which, pair],
            n_recv.at[which, pair],
            neighbours[which],
        )

    def project(pair):
        hand(2 * pair + 1 - core).wait_recv()
        states = xg[pl.ds(2 * pair, 2)].reshape(2 * own, D).astype(F32)
        inverse = lax.rsqrt(jnp.sum(states * states, axis=1, keepdims=True) / D + EPS)
        scaled = (states * gain_v[...]).astype(BF16)
        totals = jnp.dot(scaled, win_t[...], preferred_element_type=F32) * inverse
        start = pl.multiple_of(pair * 2 * own, 2 * own)
        query = totals[:, :wide].astype(BF16).astype(F32) * (1.0 / math.sqrt(HEAD))
        qs[pl.ds(start, 2 * own)] = jnp.where(wide_lane < HEAD, query, 0.0).astype(BF16)
        inside = pl.multiple_of(pair % pairs * 2 * own, 2 * own)
        kvx[blocks_here + pair // pairs, pl.ds(inside, 2 * own)] = totals[:, HEAD:].astype(BF16)

    def share_keys(pair):
        for which in range(2):
            n_copy(pair, which).start()

    last = ring // 2
    half = own // 2
    own_half = pl.ds(pl.multiple_of(core * half, half), half)
    other_half = pl.ds(pl.multiple_of((1 - core) * half, half), half)
    weights_sent = []

    def w_send_to(source, at, to):
        copy = remote(
            source, woutg.at[at, own_half], w_send.at[len(weights_sent)], w_recv.at[at], to
        )
        copy.start()
        weights_sent.append(copy)

    def w_wait(at):
        part_of = woutg.at[at, own_half]
        remote(part_of, part_of, w_send.at[0], w_recv.at[at], up).wait_recv()

    def c_copy(at, side):
        part_of = woutg.at[at, side]
        return remote(part_of, part_of, c_send.at[at], c_recv.at[at], twin)

    def weight_ring():
        mine = wout_ref.at[own_half]
        for to in (up, down, across):
            w_send_to(mine, t, to)
        yield
        at = 2 * y + 1 - xh
        w_wait(at)
        for to in (up, down):
            w_send_to(woutg.at[at, own_half], at, to)
        c_copy(at, own_half).start()
        yield
        for k in range(1, last + 1):
            for column in range(2):
                side = xh if column == 0 else 1 - xh
                for way, to in ((-k, up), (k, down)):
                    turned = column == 0 if way < 0 else column == 1
                    if k == last and not turned:
                        continue
                    at = 2 * mate(way) + side
                    w_wait(at)
                    if k < last - 1 or (k == last - 1 and turned):
                        w_send_to(woutg.at[at, own_half], at, to)
                    c_copy(at, own_half).start()
            yield

    weight_steps = weight_ring()

    for k in range(1, last):
        below, above = 2 * mate(-k) + core, 2 * mate(k) + core
        for c in range(CHUNKS):
            x_wait(below, c)
            if k < last - 1 or c < CHUNKS // 2:
                x_forward(below, c, up)
            x_wait(above, c)
            if k < last - 1 or c >= CHUNKS // 2:
                x_forward(above, c, down)
        hand(below).start()
        hand(above).start()
        if k == 2:
            local(win_ref, win_v, g_sem.at[0]).wait()
            win_t[...] = jnp.transpose(win_v[...].astype(F32)).astype(BF16)
            project(y)

    next(weight_steps)

    @pl.when(has_higher)
    def _():
        pl.semaphore_wait(ready, (planes - 1 - z) * 4)

    @pl.loop(0, parts)
    def _(i):
        @pl.when(i != self_slot)
        def _():
            r_copy(i, behind(i)).start()

    reqr[self_slot] = reqs[self_slot]
    share_keys(y)
    for near in range(1, last - 1):
        for pair in (mate(-near), mate(near)):
            project(pair)
            share_keys(pair)
    opposite = 2 * mate(last) + core
    for c in range(CHUNKS):
        x_wait(opposite, c)
    hand(opposite).start()
    for pair in (mate(1 - last), mate(last - 1), mate(last)):
        project(pair)
        share_keys(pair)


    diagonal = iota((128, 128), 0) == iota((128, 128), 1)
    lane_index = iota((128, rows), 1).astype(F32)

    def one_hot(row):
        column = jnp.sum(jnp.where(diagonal, row, 0.0), axis=1, keepdims=True)
        return jnp.where(lane_index == column, 1.0, 0.0).astype(BF16)

    def e_copy(i, to):
        return remote(snd.at[i], rcv.at[:, i], e_send.at[i], e_recv.at[i], to)

    batch = 4

    def pick(step):
        table = kvx[blocks_here : 2 * blocks_here].reshape(rows, wide)
        chosen = [one_hot(reqr[step * batch + j]) for j in range(batch)]
        got = jnp.dot(jnp.concatenate(chosen, axis=0), table, preferred_element_type=F32)
        snd[pl.ds(step * batch, batch)] = got.astype(BF16).reshape(batch, ROUNDS, per, wide)

    def serve(turn):
        swing = (turn + 1) // 2 * (1 - turn % 2 * 2) * (1 - 2 * core)
        step = (planes // 2 + swing + planes) % planes
        for j in range(batch):
            i = step * batch + j

            @pl.when(i != self_slot)
            def _():
                r_copy(i, ahead(i)).wait_recv()

        pick(step)
        for j in range(batch):
            i = step * batch + j

            @pl.when(i != self_slot)
            def _():
                e_copy(i, ahead(i)).start()

    @pl.loop(0, 5)
    def _(turn):
        serve(turn)

    next(weight_steps)

    @pl.loop(5, planes)
    def _(turn):
        serve(turn)

    rcv[:, self_slot] = snd[self_slot]

    next(weight_steps)
    for part_of in range(2):

        @pl.loop(part_of * ROUNDS * row_chunks // 2, (part_of + 1) * ROUNDS * row_chunks // 2)
        def _(i):
            span = pl.ds(pl.multiple_of(i % row_chunks * 128, 128), 128)
            place[i // row_chunks, span] = one_hot(posr[i])

        next(weight_steps)

    @pl.when(jnp.logical_not(home))
    def _():
        cross_b.wait_recv()
        twin_b.wait_recv()

    blocks_copy = pltpu.make_async_copy(blocks_v, blocks_s, l_sem.at[3])
    blocks_copy.start()
    blocks_copy.wait()
    for pair in range(ring):
        for which in range(2):
            n_copy(pair, which).wait_recv()
    for b in range(blocks_here):
        span = slice(b * BLOCK, (b + 1) * BLOCK)
        query = qs[span]
        scores = []
        keys = []
        for j in range(NEIGH):
            at = blocks_s[b, j] - part * blocks_here + blocks_here
            at = jnp.minimum(jnp.maximum(at, 0), 3 * blocks_here - 1)
            block = kvx[at]
            keys.append(block)
            scores.append(lax.dot_general(query, block, NT, preferred_element_type=F32))
        top = functools.reduce(jnp.maximum, scores)
        top = jnp.max(top, axis=1, keepdims=True)
        total = jnp.zeros((BLOCK, 1), F32)
        blended = jnp.zeros((BLOCK, wide), F32)
        for j in range(NEIGH):
            weights = jnp.exp(scores[j] - top)
            total += jnp.sum(weights, axis=1, keepdims=True)
            blended += jnp.dot(weights.astype(BF16), keys[j], preferred_element_type=F32)
        oloc[span] = blended
        mloc[span] = jnp.broadcast_to(top, (BLOCK, wide))
        lloc[span] = jnp.broadcast_to(total, (BLOCK, wide))
        next(weight_steps, None)


    @pl.loop(0, parts)
    def _(i):
        @pl.when(i != self_slot)
        def _():
            e_copy(i, behind(i)).wait_recv()

    left = iota((half, wide), 1) < HEAD
    share = BLOCK // own

    def a_copy(i, at):
        return remote(
            atts.at[i], attr.at[head], a_send.at[i], a_recv.at[head], device(part, at)
        )

    def a_wait(at):
        remote(atts.at[0], attr.at[at], a_send.at[0], a_recv.at[at], up).wait_recv()

    owners = []
    for turned in (2, 1, 3, 0):
        b = (t // share + turned) % blocks_here
        span = pl.ds(pl.multiple_of(b * BLOCK, BLOCK), BLOCK)
        far = [
            jnp.dot(place[r, span], rcv[r].reshape(rows, wide), preferred_element_type=F32)
            for r in range(ROUNDS)
        ]
        query = qs[span].astype(F32)
        top = mloc[span]
        edges = []
        for r in range(ROUNDS):
            score = jnp.sum(query * far[r], axis=1, keepdims=True)
            edges.append(jnp.broadcast_to(score, (BLOCK, wide)) + bias_v[r : r + 1])
        new_top = functools.reduce(jnp.maximum, edges, top)
        keep = jnp.exp(top - new_top)
        total = lloc[span] * keep
        blended = oloc[span] * keep
        for r in range(ROUNDS):
            weight = jnp.exp(edges[r] - new_top)
            total += weight
            blended += weight.astype(BF16).astype(F32) * far[r]
        attended = blended / total
        for s in range(share):
            i, at = len(owners), share * b + s
            owners.append(at)
            upper = attended[s * own : s * own + half]
            lower = attended[s * own + half : (s + 1) * own]
            atts[i] = jnp.where(left, pltpu.roll(upper, HEAD, 1), lower).astype(BF16)
            if turned:
                a_copy(i, at).start()
            else:
                here = jnp.logical_and(home, at == t)

                @pl.when(here)
                def _():
                    attr[head] = atts[i]

                @pl.when(jnp.logical_not(here))
                def _():
                    a_copy(i, at).start()

    for at in range(peers):

        @pl.when(at != t)
        def _():
            c_copy(at, other_half).wait_recv()

    wout_in.wait()
    x_in.wait()
    for at in range(peers):

        @pl.when(jnp.logical_or(at != head, jnp.logical_not(home)))
        def _():
            a_wait(at)

    tops, bottoms = [], []
    for pair in range(peers // 2):
        even = attr[2 * pair].astype(F32)
        odd = attr[2 * pair + 1].astype(F32)
        tops.append(jnp.where(left, even, pltpu.roll(odd, HEAD, 1)).astype(BF16))
        bottoms.append(jnp.where(left, pltpu.roll(even, HEAD, 1), odd).astype(BF16))
    attended = jnp.concatenate(
        [jnp.concatenate(tops, axis=1), jnp.concatenate(bottoms, axis=1)], axis=0
    )
    result = jnp.dot(attended, woutg[...].reshape(peers * own, D), preferred_element_type=F32)
    out_ref[...] = (xown[...].astype(F32) + result).astype(BF16)

    @pl.when(jnp.logical_not(home))
    def _():
        for c in range(CHUNKS):
            for to in range(3):
                swap_x(c, to).wait_send()
        cross_w.wait_send()
        cross_b.wait_send()

    @pl.when(home)
    def _():
        twin_s.wait_send()
        twin_b.wait_send()
        for c in range(CHUNKS):
            for to in range(2):
                lead(c, to).wait_send()

    for copy in sent + weights_sent:
        copy.wait_send()
    for pair in range(ring):
        for which in range(2):
            n_copy(pair, which).wait_send()

    @pl.loop(0, parts)
    def _(i):
        @pl.when(i != self_slot)
        def _():
            r_copy(i, behind(i)).wait_send()
            e_copy(i, ahead(i)).wait_send()

    for k in range(ring):
        hand(2 * k + core).wait_send()
    for i, at in enumerate(owners):

        @pl.when(jnp.logical_or(at != t, jnp.logical_not(home)))
        def _():
            a_copy(i, at).wait_send()

    for at in range(peers):

        @pl.when(at != t)
        def _():
            c_copy(at, own_half).wait_send()


def per_device(
    node_states,
    norm_gain,
    input_weight,
    output_weight,
    expander_bias,
    local_blocks,
    expander_source,
):
    parts = lax.axis_size("nodes")
    peers = lax.axis_size("tensor")
    own = node_states.shape[0]
    rows = own * peers
    per = rows // parts
    chunks = rows // 128
    wide = 2 * HEAD
    blocks_here = rows // BLOCK
    dma = pltpu.SemaphoreType.DMA
    vmem = pltpu.VMEM
    return pl.pallas_call(
        functools.partial(kernel, parts, peers),
        out_shape=jax.ShapeDtypeStruct((own, D), BF16),
        in_specs=[pl.BlockSpec(memory_space=pltpu.HBM)] * 7,
        out_specs=pl.BlockSpec(memory_space=pltpu.VMEM),
        scratch_shapes=[
            vmem((own, D), BF16),
            vmem((1, D), F32),
            vmem((3 * HEAD, D), BF16),
            vmem((D, 3 * HEAD), BF16),
            vmem((1, ROUNDS), F32),
            vmem((8, 128), F32),
            vmem((8, 128), F32),
            vmem((blocks_here, NEIGH), I32),
            vmem((8, 128), I32),
            vmem((8, 128), I32),
            pltpu.SMEM((8, 128), I32),
            vmem((ROUNDS, rows), I32),
            vmem((peers, own, D), BF16),
            vmem((3 * blocks_here, BLOCK, wide), BF16),
            vmem((rows, wide), BF16),
            vmem((parts, 1, ROUNDS * per), F32),
            vmem((parts, 1, ROUNDS * per), F32),
            vmem((ROUNDS * chunks, 1, 128), F32),
            vmem((ROUNDS, rows, rows), BF16),
            vmem((parts, ROUNDS, per, wide), BF16),
            vmem((ROUNDS, parts, per, wide), BF16),
            vmem((rows, wide), F32),
            vmem((rows, wide), F32),
            vmem((rows, wide), F32),
            vmem((peers, own // 2, wide), BF16),
            vmem((peers, own // 2, wide), BF16),
            vmem((peers, own, D), BF16),
            dma((5,)),
            dma((3 * CHUNKS + 2,)),
            dma((4,)),
            dma((8 * CHUNKS,)),
            dma((peers, CHUNKS)),
            dma((peers // 2,)),
            dma((peers // 2,)),
            dma((peers,)),
            dma((peers,)),
            dma((peers,)),
            dma((peers,)),
            dma((parts,)),
            dma((parts,)),
            dma((parts,)),
            dma((parts,)),
            dma((2, peers // 2)),
            dma((2, peers // 2)),
            dma((peers,)),
            dma((peers,)),
            pltpu.SemaphoreType.REGULAR,
            pltpu.SemaphoreType.REGULAR,
        ],
        compiler_params=pltpu.CompilerParams(
            collective_id=0, has_side_effects=True, vmem_limit_bytes=58 * 1024 * 1024
        ),
        cost_estimate=pl.CostEstimate(
            flops=2 * rows * D * 8 * HEAD, bytes_accessed=4 * own * D * 8, transcendentals=rows * rows
        ),
    )(
        node_states,
        norm_gain.reshape(1, D),
        input_weight,
        output_weight,
        jnp.transpose(expander_bias),
        local_blocks,
        expander_source,
    )


def solution(mesh):
    in_specs = (
        P(("nodes", "tensor"), None),
        P(),
        P("tensor", None),
        P("tensor", None),
        P(None, "tensor"),
        P("nodes", None),
        P(None, "nodes"),
    )
    out_specs = P(("nodes", "tensor"), None)
    return jax.shard_map(
        per_device, mesh=mesh, in_specs=in_specs, out_specs=out_specs, check_vma=False
    )
```

```python
import functools
import math

import jax
import jax.numpy as jnp
from jax import lax
from jax.experimental import pallas as pl
from jax.experimental.pallas import tpu as pltpu
from jax.sharding import PartitionSpec as P

D = 1024
HEAD = 64
BLOCK = 256
NEIGH = 4
ROUNDS = 4
EPS = 1e-05
CHUNKS = 2

BF16 = jnp.bfloat16
F32 = jnp.float32
I32 = jnp.int32
MESH = pl.DeviceIdType.MESH
NT = (((1,), (1,)), ((), ()))


def iota(shape, dim):
    return lax.broadcasted_iota(I32, shape, dim)


def kernel(
    parts,
    peers,
    x_ref,
    gain_ref,
    win_ref,
    wout_ref,
    bias_ref,
    blocks_ref,
    src_ref,
    out_ref,
    xown,
    gain_v,
    win_v,
    win_t,
    bias_in,
    bias_out,
    bias_v,
    blocks_in,
    blocks_out,
    blocks_v,
    blocks_s,
    src_v,
    xg,
    kvx,
    qs,
    reqs,
    reqr,
    posr,
    place,
    snd,
    rcv,
    oloc,
    mloc,
    lloc,
    atts,
    attr,
    woutg,
    l_sem,
    s_sem,
    g_sem,
    x_send,
    x_recv,
    h_send,
    h_recv,
    w_send,
    w_recv,
    c_send,
    c_recv,
    r_send,
    r_recv,
    e_send,
    e_recv,
    n_send,
    n_recv,
    a_send,
    a_recv,
    token,
    ready,
):
    own = x_ref.shape[0]
    rows = own * peers
    ring = peers // 2
    per = rows // parts
    blocks_here = rows // BLOCK
    wide = 2 * HEAD
    row_chunks = rows // 128
    p = lax.axis_index("nodes")
    t = lax.axis_index("tensor")
    core = p % 2
    base = p - core
    y, xh = t // 2, t % 2
    part = base + xh
    head = 2 * y + core
    home = core == xh

    def device(nodes, tensor):
        return {"nodes": nodes, "tensor": tensor}

    def worker(partition):
        return device(partition - partition % 2 + core, y * 2 + partition % 2)

    planes = parts // 4
    xl, z = p // (parts // 2), p // 2 % planes

    def shifted(i, plane):
        lo, hi = i % 4 // 2, i % 2
        return worker((xl + lo) % 2 * (parts // 2) + plane % planes * 2 + (xh + hi) % 2)

    def ahead(i):
        return shifted(i, z + i // 4)

    def behind(i):
        return shifted(i, z + planes - i // 4)

    self_slot = 0
    up = device(p, ((y + 1) % ring) * 2 + xh)
    down = device(p, ((y + ring - 1) % ring) * 2 + xh)
    twin = device(base + 1 - core, t)
    swap = device(base + 1 - core, y * 2 + 1 - xh)
    swap_up = device(base + 1 - core, ((y + 1) % ring) * 2 + 1 - xh)
    swap_down = device(base + 1 - core, ((y + ring - 1) % ring) * 2 + 1 - xh)
    cross = device((base + parts // 2) % parts + 1 - core, y * 2 + 1 - xh)
    across = device((p + parts // 2) % parts, y * 2 + 1 - xh)

    x_in = pltpu.make_async_copy(x_ref, xown, l_sem.at[0])
    gain_in = pltpu.make_async_copy(gain_ref, gain_v, l_sem.at[1])
    bias_load = pltpu.make_async_copy(bias_ref, bias_in, l_sem.at[2])
    blocks_load = pltpu.make_async_copy(blocks_ref, blocks_in, l_sem.at[3])
    wout_in = pltpu.make_async_copy(wout_ref, woutg.at[t], l_sem.at[4])
    for copy in (bias_load, blocks_load, gain_in, x_in, wout_in):
        copy.start()

    def local(source, target, sem):
        return pltpu.make_async_copy(source, target, sem)

    def remote(source, target, send, recv, to):
        return pltpu.make_async_remote_copy(
            src_ref=source,
            dst_ref=target,
            send_sem=send,
            recv_sem=recv,
            device_id=to,
            device_id_type=MESH,
        )

    chunk = own // CHUNKS

    def piece(at, c):
        return xg.at[at, pl.ds(c * chunk, chunk)]

    @pl.when(home)
    def _():
        for c in range(CHUNKS):
            local(x_ref.at[pl.ds(c * chunk, chunk)], piece(t, c), x_recv.at[t, c]).start()
        local(win_ref, win_v, g_sem.at[0]).start()
        local(src_ref, src_v, g_sem.at[1]).start()

    barrier = pltpu.get_barrier_semaphore()

    def greet(to):
        pl.semaphore_signal(barrier, inc=1, device_id=to, device_id_type=MESH)

    for to in (up, down, twin, swap, swap_up, swap_down, cross, ahead(1), ahead(2), ahead(3)):
        greet(to)
    higher, lower = ahead(4), behind(4)
    has_higher, has_lower = z < planes - 1, z > 0

    @pl.when(has_higher)
    def _():
        greet(higher)

    @pl.when(has_lower)
    def _():
        greet(lower)

    bias_load.wait()
    for r in range(ROUNDS):
        bias_out[r : r + 1] = jnp.broadcast_to(bias_in[:, r : r + 1], (1, 128))
    blocks_load.wait()
    blocks_out[0:blocks_here, 0:NEIGH] = blocks_in[...]

    @pl.when(home)
    def _():
        bias_v[...] = bias_out[...]
        blocks_v[...] = blocks_out[...]

    pl.semaphore_wait(barrier, 10 + jnp.minimum(z, 1) + jnp.minimum(planes - 1 - z, 1))

    def swap_x(c, to):
        return remote(
            x_ref.at[pl.ds(c * chunk, chunk)],
            piece(t, c),
            s_sem.at[to * CHUNKS + c],
            x_recv.at[t, c],
            (swap, swap_up, swap_down)[to],
        )

    cross_w = remote(win_ref, win_v, s_sem.at[3 * CHUNKS], g_sem.at[0], cross)
    cross_b = remote(bias_out, bias_v, s_sem.at[3 * CHUNKS + 1], g_sem.at[2], cross)
    twin_s = remote(src_ref, src_v, s_sem.at[3 * CHUNKS], g_sem.at[1], twin)
    twin_b = remote(blocks_out, blocks_v, s_sem.at[3 * CHUNKS + 1], g_sem.at[3], twin)

    @pl.when(jnp.logical_not(home))
    def _():
        for c in range(CHUNKS):
            for to in (1, 2, 0):
                swap_x(c, to).start()
        cross_w.start()
        cross_b.start()

    @pl.when(home)
    def _():
        twin_s.start()
        twin_b.start()

    sent = []

    def x_forward(at, c, to):
        copy = remote(piece(at, c), piece(at, c), x_send.at[len(sent)], x_recv.at[at, c], to)
        copy.start()
        sent.append(copy)

    def x_wait(at, c):
        remote(piece(at, c), piece(at, c), x_send.at[0], x_recv.at[at, c], up).wait_recv()

    def hand(at):
        return remote(xg.at[at], xg.at[at], h_send.at[at // 2], h_recv.at[at // 2], twin)

    def mate(k):
        return (y + ring + k) % ring

    first = 2 * y + core

    def lead(c, to):
        start = x_ref.at[pl.ds(c * chunk, chunk)]
        return remote(
            start, piece(t, c), s_sem.at[2 * c + to], x_recv.at[t, c], (up, down)[to]
        )

    @pl.when(home)
    def _():
        for c in range(CHUNKS):
            for to in range(2):
                lead(c, to).start()

    @pl.when(has_lower)
    def _():
        pl.semaphore_wait(token, 1)

    @pl.when(has_higher)
    def _():
        pl.semaphore_signal(token, inc=1, device_id=higher, device_id_type=MESH)

    @pl.loop(0, parts)
    def _(i):
        @pl.when(jnp.logical_and(i >= 4, i // 4 <= z))
        def _():
            pl.semaphore_signal(ready, inc=1, device_id=behind(i), device_id_type=MESH)

    for c in range(CHUNKS):
        x_wait(first, c)
    hand(first).start()

    local(src_ref, src_v, g_sem.at[1]).wait()
    src = src_v[...]
    owner = lax.shift_right_logical(src, rows.bit_length() - 1)
    within = (src & (rows - 1)).astype(F32)
    owner_plane = lax.shift_right_logical(owner, 1) & (planes - 1)
    owner_lo = lax.shift_right_logical(owner, (parts // 2).bit_length() - 1)
    slot = (
        ((z + planes - owner_plane) & (planes - 1)) * 4
        + ((owner_lo + xl) & 1) * 2
        + ((owner + xh) & 1)
    )
    high = jnp.floor(within * (1.0 / per))
    low = within - high * per
    slot_rows = iota((parts, rows), 0)
    belongs = [slot[r : r + 1] == slot_rows for r in range(ROUNDS)]
    before = jnp.where(iota((rows, rows), 0) < iota((rows, rows), 1), 1.0, 0.0).astype(BF16)
    member = jnp.concatenate([jnp.where(b, 1.0, 0.0) for b in belongs], axis=0).astype(BF16)
    counts = jnp.dot(member, before, preferred_element_type=F32)
    entry = iota((ROUNDS * per, rows), 0).astype(F32)
    wanted_high = jnp.zeros((parts, ROUNDS * per), F32)
    wanted_low = jnp.zeros((parts, ROUNDS * per), F32)
    for r in range(ROUNDS):
        rank = jnp.sum(
            jnp.where(belongs[r], counts[r * parts : (r + 1) * parts], 0.0), axis=0, keepdims=True
        )
        position = slot[r : r + 1].astype(F32) * per + rank
        for c in range(row_chunks):
            posr[r * row_chunks + c] = position[:, c * 128 : (c + 1) * 128]
        chosen = jnp.where(entry == rank + r * per, 1.0, 0.0).astype(BF16)
        wanted_high += lax.dot_general(
            jnp.where(belongs[r], high[r : r + 1], 0.0).astype(BF16),
            chosen,
            NT,
            preferred_element_type=F32,
        )
        wanted_low += lax.dot_general(
            jnp.where(belongs[r], low[r : r + 1], 0.0).astype(BF16),
            chosen,
            NT,
            preferred_element_type=F32,
        )
    wanted = wanted_high * per + wanted_low
    for i in range(parts):
        reqs[i] = wanted[i : i + 1]

    def r_copy(i, to):
        return remote(reqs.at[i], reqr.at[i], r_send.at[i], r_recv.at[i], to)

    gain_in.wait()
    wide_lane = iota((2 * own, wide), 1)
    pairs = BLOCK // (2 * own)
    neighbours = (worker((part + 1) % parts), worker((part + parts - 1) % parts))

    def n_copy(pair, which):
        inside = pl.ds(pl.multiple_of(pair % pairs * 2 * own, 2 * own), 2 * own)
        return remote(
            kvx.at[blocks_here + pair // pairs, inside],
            kvx.at[2 * blocks_here * which + pair // pairs, inside],
            n_send.at[which, pair],
            n_recv.at[which, pair],
            neighbours[which],
        )

    def project(pair):
        hand(2 * pair + 1 - core).wait_recv()
        states = xg[pl.ds(2 * pair, 2)].reshape(2 * own, D).astype(F32)
        inverse = lax.rsqrt(jnp.sum(states * states, axis=1, keepdims=True) / D + EPS)
        scaled = (states * gain_v[...]).astype(BF16)
        totals = jnp.dot(scaled, win_t[...], preferred_element_type=F32) * inverse
        start = pl.multiple_of(pair * 2 * own, 2 * own)
        query = totals[:, :wide].astype(BF16).astype(F32) * (1.0 / math.sqrt(HEAD))
        qs[pl.ds(start, 2 * own)] = jnp.where(wide_lane < HEAD, query, 0.0).astype(BF16)
        inside = pl.multiple_of(pair % pairs * 2 * own, 2 * own)
        kvx[blocks_here + pair // pairs, pl.ds(inside, 2 * own)] = totals[:, HEAD:].astype(BF16)

    def share_keys(pair):
        for which in range(2):
            n_copy(pair, which).start()

    last = ring // 2
    half = own // 2
    own_half = pl.ds(pl.multiple_of(core * half, half), half)
    other_half = pl.ds(pl.multiple_of((1 - core) * half, half), half)
    weights_sent = []

    def w_send_to(source, at, to):
        copy = remote(
            source, woutg.at[at, own_half], w_send.at[len(weights_sent)], w_recv.at[at], to
        )
        copy.start()
        weights_sent.append(copy)

    def w_wait(at):
        part_of = woutg.at[at, own_half]
        remote(part_of, part_of, w_send.at[0], w_recv.at[at], up).wait_recv()

    def c_copy(at, side):
        part_of = woutg.at[at, side]
        return remote(part_of, part_of, c_send.at[at], c_recv.at[at], twin)

    def weight_ring():
        mine = wout_ref.at[own_half]
        for to in (up, down, across):
            w_send_to(mine, t, to)
        yield
        at = 2 * y + 1 - xh
        w_wait(at)
        for to in (up, down):
            w_send_to(woutg.at[at, own_half], at, to)
        c_copy(at, own_half).start()
        yield
        for k in range(1, last + 1):
            for column in range(2):
                side = xh if column == 0 else 1 - xh
                for way, to in ((-k, up), (k, down)):
                    turned = column == 0 if way < 0 else column == 1
                    if k == last and not turned:
                        continue
                    at = 2 * mate(way) + side
                    w_wait(at)
                    if k < last - 1 or (k == last - 1 and turned):
                        w_send_to(woutg.at[at, own_half], at, to)
                    c_copy(at, own_half).start()
            yield

    weight_steps = weight_ring()

    for k in range(1, last):
        below, above = 2 * mate(-k) + core, 2 * mate(k) + core
        for c in range(CHUNKS):
            x_wait(below, c)
            if k < last - 1 or c < CHUNKS // 2:
                x_forward(below, c, up)
            x_wait(above, c)
            if k < last - 1 or c >= CHUNKS // 2:
                x_forward(above, c, down)
        hand(below).start()
        hand(above).start()
        if k == 2:

            @pl.when(has_higher)
            def _():
                pl.semaphore_wait(ready, (planes - 1 - z) * 4)

            @pl.loop(0, parts)
            def _(i):
                @pl.when(i != self_slot)
                def _():
                    r_copy(i, behind(i)).start()

            reqr[self_slot] = reqs[self_slot]

            local(win_ref, win_v, g_sem.at[0]).wait()
            win_t[...] = jnp.transpose(win_v[...].astype(F32)).astype(BF16)
            project(y)

    next(weight_steps)

    share_keys(y)
    for near in range(1, last - 1):
        for pair in (mate(-near), mate(near)):
            project(pair)
            share_keys(pair)
    opposite = 2 * mate(last) + core
    for c in range(CHUNKS):
        x_wait(opposite, c)
    hand(opposite).start()
    for pair in (mate(1 - last), mate(last - 1), mate(last)):
        project(pair)
        share_keys(pair)


    diagonal = iota((128, 128), 0) == iota((128, 128), 1)
    lane_index = iota((128, rows), 1).astype(F32)

    def one_hot(row):
        column = jnp.sum(jnp.where(diagonal, row, 0.0), axis=1, keepdims=True)
        return jnp.where(lane_index == column, 1.0, 0.0).astype(BF16)

    def e_copy(i, to):
        return remote(snd.at[i], rcv.at[:, i], e_send.at[i], e_recv.at[i], to)

    batch = 4

    def pick(step):
        table = kvx[blocks_here : 2 * blocks_here].reshape(rows, wide)
        chosen = [one_hot(reqr[step * batch + j]) for j in range(batch)]
        got = jnp.dot(jnp.concatenate(chosen, axis=0), table, preferred_element_type=F32)
        snd[pl.ds(step * batch, batch)] = got.astype(BF16).reshape(batch, ROUNDS, per, wide)

    def serve(turn):
        swing = (turn + 1) // 2 * (1 - turn % 2 * 2) * (1 - 2 * core)
        step = (planes // 2 + swing + planes) % planes
        for j in range(batch):
            i = step * batch + j

            @pl.when(i != self_slot)
            def _():
                r_copy(i, ahead(i)).wait_recv()

        pick(step)
        for j in range(batch):
            i = step * batch + j

            @pl.when(i != self_slot)
            def _():
                e_copy(i, ahead(i)).start()

    @pl.loop(0, 5)
    def _(turn):
        serve(turn)

    next(weight_steps)

    @pl.loop(5, planes)
    def _(turn):
        serve(turn)

    rcv[:, self_slot] = snd[self_slot]

    next(weight_steps)
    for part_of in range(2):

        @pl.loop(part_of * ROUNDS * row_chunks // 2, (part_of + 1) * ROUNDS * row_chunks // 2)
        def _(i):
            span = pl.ds(pl.multiple_of(i % row_chunks * 128, 128), 128)
            place[i // row_chunks, span] = one_hot(posr[i])

        next(weight_steps)

    @pl.when(jnp.logical_not(home))
    def _():
        cross_b.wait_recv()
        twin_b.wait_recv()

    blocks_copy = pltpu.make_async_copy(blocks_v, blocks_s, l_sem.at[3])
    blocks_copy.start()
    blocks_copy.wait()
    for pair in range(ring):
        for which in range(2):
            n_copy(pair, which).wait_recv()
    for b in range(blocks_here):
        span = slice(b * BLOCK, (b + 1) * BLOCK)
        query = qs[span]
        scores = []
        keys = []
        for j in range(NEIGH):
            at = blocks_s[b, j] - part * blocks_here + blocks_here
            at = jnp.minimum(jnp.maximum(at, 0), 3 * blocks_here - 1)
            block = kvx[at]
            keys.append(block)
            scores.append(lax.dot_general(query, block, NT, preferred_element_type=F32))
        top = functools.reduce(jnp.maximum, scores)
        top = jnp.max(top, axis=1, keepdims=True)
        total = jnp.zeros((BLOCK, 1), F32)
        blended = jnp.zeros((BLOCK, wide), F32)
        for j in range(NEIGH):
            weights = jnp.exp(scores[j] - top)
            total += jnp.sum(weights, axis=1, keepdims=True)
            blended += jnp.dot(weights.astype(BF16), keys[j], preferred_element_type=F32)
        oloc[span] = blended
        mloc[span] = jnp.broadcast_to(top, (BLOCK, wide))
        lloc[span] = jnp.broadcast_to(total, (BLOCK, wide))
        next(weight_steps, None)


    @pl.loop(0, parts)
    def _(i):
        @pl.when(i != self_slot)
        def _():
            e_copy(i, behind(i)).wait_recv()

    left = iota((half, wide), 1) < HEAD
    share = BLOCK // own

    def a_copy(i, at):
        return remote(
            atts.at[i], attr.at[head], a_send.at[i], a_recv.at[head], device(part, at)
        )

    def a_wait(at):
        remote(atts.at[0], attr.at[at], a_send.at[0], a_recv.at[at], up).wait_recv()

    owners = []
    for turned in (2, 1, 3, 0):
        b = (t // share + turned) % blocks_here
        span = pl.ds(pl.multiple_of(b * BLOCK, BLOCK), BLOCK)
        far = [
            jnp.dot(place[r, span], rcv[r].reshape(rows, wide), preferred_element_type=F32)
            for r in range(ROUNDS)
        ]
        query = qs[span].astype(F32)
        top = mloc[span]
        edges = []
        for r in range(ROUNDS):
            score = jnp.sum(query * far[r], axis=1, keepdims=True)
            edges.append(jnp.broadcast_to(score, (BLOCK, wide)) + bias_v[r : r + 1])
        new_top = functools.reduce(jnp.maximum, edges, top)
        keep = jnp.exp(top - new_top)
        total = lloc[span] * keep
        blended = oloc[span] * keep
        for r in range(ROUNDS):
            weight = jnp.exp(edges[r] - new_top)
            total += weight
            blended += weight.astype(BF16).astype(F32) * far[r]
        attended = blended / total
        for s in range(share):
            i, at = len(owners), share * b + s
            owners.append(at)
            upper = attended[s * own : s * own + half]
            lower = attended[s * own + half : (s + 1) * own]
            atts[i] = jnp.where(left, pltpu.roll(upper, HEAD, 1), lower).astype(BF16)
            if turned:
                a_copy(i, at).start()
            else:
                here = jnp.logical_and(home, at == t)

                @pl.when(here)
                def _():
                    attr[head] = atts[i]

                @pl.when(jnp.logical_not(here))
                def _():
                    a_copy(i, at).start()

    for at in range(peers):

        @pl.when(at != t)
        def _():
            c_copy(at, other_half).wait_recv()

    wout_in.wait()
    x_in.wait()
    for at in range(peers):

        @pl.when(jnp.logical_or(at != head, jnp.logical_not(home)))
        def _():
            a_wait(at)

    tops, bottoms = [], []
    for pair in range(peers // 2):
        even = attr[2 * pair].astype(F32)
        odd = attr[2 * pair + 1].astype(F32)
        tops.append(jnp.where(left, even, pltpu.roll(odd, HEAD, 1)).astype(BF16))
        bottoms.append(jnp.where(left, pltpu.roll(even, HEAD, 1), odd).astype(BF16))
    attended = jnp.concatenate(
        [jnp.concatenate(tops, axis=1), jnp.concatenate(bottoms, axis=1)], axis=0
    )
    result = jnp.dot(attended, woutg[...].reshape(peers * own, D), preferred_element_type=F32)
    out_ref[...] = (xown[...].astype(F32) + result).astype(BF16)

    @pl.when(jnp.logical_not(home))
    def _():
        for c in range(CHUNKS):
            for to in range(3):
                swap_x(c, to).wait_send()
        cross_w.wait_send()
        cross_b.wait_send()

    @pl.when(home)
    def _():
        twin_s.wait_send()
        twin_b.wait_send()
        for c in range(CHUNKS):
            for to in range(2):
                lead(c, to).wait_send()

    for copy in sent + weights_sent:
        copy.wait_send()
    for pair in range(ring):
        for which in range(2):
            n_copy(pair, which).wait_send()

    @pl.loop(0, parts)
    def _(i):
        @pl.when(i != self_slot)
        def _():
            r_copy(i, behind(i)).wait_send()
            e_copy(i, ahead(i)).wait_send()

    for k in range(ring):
        hand(2 * k + core).wait_send()
    for i, at in enumerate(owners):

        @pl.when(jnp.logical_or(at != t, jnp.logical_not(home)))
        def _():
            a_copy(i, at).wait_send()

    for at in range(peers):

        @pl.when(at != t)
        def _():
            c_copy(at, own_half).wait_send()


def per_device(
    node_states,
    norm_gain,
    input_weight,
    output_weight,
    expander_bias,
    local_blocks,
    expander_source,
):
    parts = lax.axis_size("nodes")
    peers = lax.axis_size("tensor")
    own = node_states.shape[0]
    rows = own * peers
    per = rows // parts
    chunks = rows // 128
    wide = 2 * HEAD
    blocks_here = rows // BLOCK
    dma = pltpu.SemaphoreType.DMA
    vmem = pltpu.VMEM
    return pl.pallas_call(
        functools.partial(kernel, parts, peers),
        out_shape=jax.ShapeDtypeStruct((own, D), BF16),
        in_specs=[pl.BlockSpec(memory_space=pltpu.HBM)] * 7,
        out_specs=pl.BlockSpec(memory_space=pltpu.VMEM),
        scratch_shapes=[
            vmem((own, D), BF16),
            vmem((1, D), F32),
            vmem((3 * HEAD, D), BF16),
            vmem((D, 3 * HEAD), BF16),
            vmem((1, ROUNDS), F32),
            vmem((8, 128), F32),
            vmem((8, 128), F32),
            vmem((blocks_here, NEIGH), I32),
            vmem((8, 128), I32),
            vmem((8, 128), I32),
            pltpu.SMEM((8, 128), I32),
            vmem((ROUNDS, rows), I32),
            vmem((peers, own, D), BF16),
            vmem((3 * blocks_here, BLOCK, wide), BF16),
            vmem((rows, wide), BF16),
            vmem((parts, 1, ROUNDS * per), F32),
            vmem((parts, 1, ROUNDS * per), F32),
            vmem((ROUNDS * chunks, 1, 128), F32),
            vmem((ROUNDS, rows, rows), BF16),
            vmem((parts, ROUNDS, per, wide), BF16),
            vmem((ROUNDS, parts, per, wide), BF16),
            vmem((rows, wide), F32),
            vmem((rows, wide), F32),
            vmem((rows, wide), F32),
            vmem((peers, own // 2, wide), BF16),
            vmem((peers, own // 2, wide), BF16),
            vmem((peers, own, D), BF16),
            dma((5,)),
            dma((3 * CHUNKS + 2,)),
            dma((4,)),
            dma((8 * CHUNKS,)),
            dma((peers, CHUNKS)),
            dma((peers // 2,)),
            dma((peers // 2,)),
            dma((peers,)),
            dma((peers,)),
            dma((peers,)),
            dma((peers,)),
            dma((parts,)),
            dma((parts,)),
            dma((parts,)),
            dma((parts,)),
            dma((2, peers // 2)),
            dma((2, peers // 2)),
            dma((peers,)),
            dma((peers,)),
            pltpu.SemaphoreType.REGULAR,
            pltpu.SemaphoreType.REGULAR,
        ],
        compiler_params=pltpu.CompilerParams(
            collective_id=0, has_side_effects=True, vmem_limit_bytes=58 * 1024 * 1024
        ),
        cost_estimate=pl.CostEstimate(
            flops=2 * rows * D * 8 * HEAD, bytes_accessed=4 * own * D * 8, transcendentals=rows * rows
        ),
    )(
        node_states,
        norm_gain.reshape(1, D),
        input_weight,
        output_weight,
        jnp.transpose(expander_bias),
        local_blocks,
        expander_source,
    )


def solution(mesh):
    in_specs = (
        P(("nodes", "tensor"), None),
        P(),
        P("tensor", None),
        P("tensor", None),
        P(None, "tensor"),
        P("nodes", None),
        P(None, "nodes"),
    )
    out_specs = P(("nodes", "tensor"), None)
    return jax.shard_map(
        per_device, mesh=mesh, in_specs=in_specs, out_specs=out_specs, check_vma=False
    )
```
